256 devices in a mesh: ctr: 8 (over x, core), comp: 32 (over y, z).
Axes of the slice: x: 4, y: 4, z: 8, core: 2. Of those that a mesh axis runs over, the one named last changes fastest.
Arguments:
- initial: float32 [64, 1024, 1024], P('ctr', 'comp'), may hold values from 0 to 2
- rates_first: float32 [1024, 1024], replicated, may hold values from 0.01 to 1
- blocks_first: int32 [16, 16], replicated, may hold values 0 or 1
- rates_second: float32 [1024, 1024], replicated, may hold values from 0.01 to 1
- blocks_second: int32 [16, 16], replicated, may hold values 0 or 1
- level_rate: float32 [64], replicated, may hold values from 30 to 300
- level_code: int32 [64], replicated, may hold values from 0 to 3
Outputs:
- transient: float32 [64, 1024, 1024], P('ctr', 'comp')
- stepped: float32 [64, 1024, 1024], P('ctr', 'comp')
The draws below stay inside these ranges and needn't reach their ends.
All inputs are finite; a program needn't handle non-finite values.
Results may differ from the reference program's by a relative error of at most 0.000071.
Values sent between devices are 32-bit elements; how exact they have to be, the bound alone decides.
No kernel may reach another device: no remote copies, remote signals or barrier semaphores. Data moves between devices by JAX's collectives and lax.ppermute only.
A program may use at most 128 MiB of HBM per device.

```python
import math
import jax
import jax.numpy as jnp
from jax import lax

ORDER = 1024
NBLK = 16
LEV = 64


def plant(result, key, smallest, largest):
    place = [jax.random.randint(jax.random.fold_in(key, axis), (), 0, length) for axis, length in enumerate(result.shape)]
    main_axis = result.shape.index(max(result.shape))
    neighbour = place[:main_axis] + [(place[main_axis] + 1) % result.shape[main_axis]] + place[main_axis + 1:]
    return result.at[tuple(place)].set(smallest).at[tuple(neighbour)].set(largest)


def level_of(stream_key, dims, split, least, top_value):
    gain = 1.0
    for position, shards_of in split:
        heights = jax.random.uniform(jax.random.fold_in(jax.random.fold_in(stream_key, 6), position), (shards_of,), jnp.float32, least / len(split), top_value / len(split))
        gain = gain * jnp.repeat(jnp.exp(heights), dims[position] // shards_of).reshape((-1,) + (1,) * (len(dims) - 1 - position))
    return gain


def setup_inputs(seed: int = 0) -> dict:
    arg_keys = jax.random.split(jax.random.key(seed), 8)
    return {
        "initial": jnp.clip(2.0 * jax.random.uniform(arg_keys[0], (LEV, ORDER, ORDER), jnp.float32) ** level_of(arg_keys[0], (LEV, ORDER, ORDER), ((0, 8), (1, 32)), -0.2, 0.2), 0.0, 2.0),
        "rates_first": jnp.clip(jnp.exp(jax.random.uniform(arg_keys[1], (ORDER, ORDER), jnp.float32, math.log(0.01), math.log(1.0))), 0.01, 1.0),
        "blocks_first": plant((jax.random.randint(arg_keys[2], (NBLK, NBLK), 0, 2) < 1).astype(jnp.int32), jax.random.fold_in(arg_keys[2], 1), 0, 1),
        "rates_second": jnp.clip(jnp.exp(jax.random.uniform(arg_keys[3], (ORDER, ORDER), jnp.float32, math.log(0.01), math.log(1.0))), 0.01, 1.0),
        "blocks_second": plant((jax.random.randint(arg_keys[4], (NBLK, NBLK), 0, 2) < 1).astype(jnp.int32), jax.random.fold_in(arg_keys[4], 1), 0, 1),
        "level_rate": jnp.clip(jnp.exp(jax.random.uniform(arg_keys[5], (LEV,), jnp.float32, math.log(30.0), math.log(300.0))), 30.0, 300.0),
        "level_code": plant(jax.random.randint(arg_keys[6], (LEV,), 0, 4), jax.random.fold_in(arg_keys[6], 1), 0, 3).astype(jnp.int32),
    }


def expand(rates, blocks):
    order = rates.shape[0]
    nblocks = blocks.shape[0]
    width = order // nblocks
    mask = jnp.broadcast_to(blocks.astype(jnp.float32)[:, None, :, None], (nblocks, width, nblocks, width)).reshape(order, order)
    full = rates * mask
    return full, jnp.sum(full, axis=1)


def reference(initial, rates_first, blocks_first, rates_second, blocks_second, level_rate, level_code):
    full_first, exits_first = expand(rates_first, blocks_first)
    full_second, exits_second = expand(rates_second, blocks_second)
    levels = level_rate.shape[0]
    hop = level_code - 2 + (level_code >= 2).astype(jnp.int32)
    target = jnp.arange(levels, dtype=jnp.int32) + hop
    live = (target >= 0) & (target < levels)
    out_rate = jnp.where(live, level_rate, jnp.float32(0.0))
    uniform_rate = jnp.max(exits_first) + jnp.max(exits_second) + jnp.max(out_rate)

    def step(state):
        order = state.shape[-1]
        first_term = jnp.dot(state.reshape(-1, order), full_first, precision=lax.Precision.HIGHEST, preferred_element_type=jnp.float32).reshape(state.shape) - state * exits_first[None, None, :]
        second_term = jnp.einsum("lnm,nk->lkm", state, full_second, precision=lax.Precision.HIGHEST, preferred_element_type=jnp.float32) - state * exits_second[None, :, None]
        padded = jnp.pad(state, ((2, 2), (0, 0), (0, 0)))
        level_term = -out_rate[:, None, None] * state
        for offset in (-2, -1, 1, 2):
            source = jnp.pad(jnp.where(hop == offset, level_rate, jnp.float32(0.0)), 2)
            level_term = level_term + source[2 - offset:2 - offset + levels][:, None, None] * padded[2 - offset:2 - offset + levels]
        return state + (first_term + second_term + level_term) / uniform_rate

    mass_one = step(initial)
    stepped = step(mass_one)
    transient = (initial + mass_one + 0.5 * stepped) / 2.5
    return transient, stepped
```

```python
import functools

import jax
import jax.numpy as jnp
from jax import lax
from jax.experimental import pallas as pl
from jax.experimental.pallas import tpu as pltpu
from jax.sharding import PartitionSpec as P

F32 = jnp.float32
BF16 = jnp.bfloat16
LANES = 256
OFFSETS = (-2, -1, 1, 2)
WHOLE = pl.BlockSpec(memory_space=pltpu.VMEM)
SCALARS = pl.BlockSpec(memory_space=pltpu.SMEM)


def params(mib):
    return pltpu.CompilerParams(vmem_limit_bytes=mib << 20)


def halves(x):
    high = x.astype(BF16)
    return high, (x - high.astype(F32)).astype(BF16)


def mm(a, b):
    return jnp.dot(a, b, preferred_element_type=F32)


def masked_rows(rates_ref, blocks_ref):
    tall, order = rates_ref.shape
    nblk = blocks_ref.shape[0]
    width = order // nblk
    first = pl.program_id(0) * (tall // width)
    row = lax.broadcasted_iota(jnp.int32, (tall, nblk), 0) // width + first
    left = (row == lax.broadcasted_iota(jnp.int32, (tall, nblk), 1)).astype(BF16)
    col = lax.broadcasted_iota(jnp.int32, (nblk, order), 1) // width
    right = (col == lax.broadcasted_iota(jnp.int32, (nblk, order), 0)).astype(BF16)
    wide = mm(blocks_ref[...].astype(F32).astype(BF16), right).astype(BF16)
    return rates_ref[...] * mm(left, wide)


def expand_kernel(turn, rates_ref, blocks_ref, high_ref, low_ref, exits_ref):
    full = masked_rows(rates_ref, blocks_ref)
    exits_ref[...] = jnp.sum(full, axis=1, keepdims=True)
    high, low = halves(full.T if turn else full)
    high_ref[...] = high
    low_ref[...] = low


def expand(rates, blocks, turn, tall=256):
    order = rates.shape[0]
    rows = pl.BlockSpec((tall, order), lambda i: (i, 0))
    out = pl.BlockSpec((order, tall), lambda i: (0, i)) if turn else rows
    return pl.pallas_call(
        functools.partial(expand_kernel, turn),
        grid=(order // tall,),
        in_specs=[rows, pl.BlockSpec(blocks.shape, lambda i: (0, 0))],
        out_specs=[out, out, pl.BlockSpec((tall, 1), lambda i: (i, 0))],
        out_shape=[
            jax.ShapeDtypeStruct((order, order), BF16),
            jax.ShapeDtypeStruct((order, order), BF16),
            jax.ShapeDtypeStruct((order, 1), F32),
        ],
        compiler_params=params(16),
        cost_estimate=pl.CostEstimate(flops=1 << 26, bytes_accessed=8 << 20, transcendentals=0),
        name="expand_turned" if turn else "expand",
    )(rates, blocks)


def turned_kernel(high_ref, low_ref, exits_ref, scale_ref, mass_ref, out_ref):
    scale = scale_ref[0]
    order = high_ref.shape[0]
    high, low = halves(mass_ref[...])
    for at in range(0, order, 256):
        rows = pl.ds(at, 256)
        left = high_ref[rows, :]
        total = mm(left, high) + mm(left, low) + mm(low_ref[rows, :], high)
        out_ref[rows, :] = (total - mass_ref[rows, :] * exits_ref[rows, :]) * scale


def turned(high, low, exits, scale, mass):
    return pl.pallas_call(
        turned_kernel,
        in_specs=[WHOLE, WHOLE, WHOLE, SCALARS, WHOLE],
        out_specs=WHOLE,
        out_shape=jax.ShapeDtypeStruct(mass.shape, F32),
        compiler_params=params(20),
        cost_estimate=pl.CostEstimate(flops=3 << 29, bytes_accessed=6 << 20, transcendentals=0),
        name="second",
    )(high, low, exits, scale, mass)


def product(x, high_ref, low_ref, cols):
    high, low = x
    return mm(high, high_ref[:, cols]) + mm(low, high_ref[:, cols]) + mm(high, low_ref[:, cols])


def hops(coef_ref, m, get, levels):
    total = None
    for k, offset in enumerate(OFFSETS):
        source = get(m - offset)
        if source is not None:
            part = coef_ref[k, m] * source
            total = part if total is None else total + part
    return total


def first_kernel(high_ref, low_ref, exits_ref, coef_ref, v_ref, below_ref, above_ref, out_ref):
    levels, rows, order = v_ref.shape
    x = halves(v_ref[...].reshape(levels * rows, order))
    scale = coef_ref[5, 0]
    for at in range(0, order, 256):
        cols = pl.ds(at, 256)
        prod = product(x, high_ref, low_ref, cols).reshape(levels, rows, 256)

        def get(n, cols=cols):
            if n < 0:
                return below_ref[n + 2, :, cols]
            if n >= levels:
                return above_ref[n - levels, :, cols]
            return v_ref[n, :, cols]

        for m in range(levels):
            here = v_ref[m, :, cols]
            change = prod[m] - here * (exits_ref[:, cols] + coef_ref[4, m])
            out_ref[m, :, cols] = here + scale * (change + hops(coef_ref, m, get, levels))


def first(high, low, exits, coef, v, below, above):
    return pl.pallas_call(
        first_kernel,
        in_specs=[WHOLE, WHOLE, WHOLE, SCALARS, WHOLE, WHOLE, WHOLE],
        out_specs=WHOLE,
        out_shape=jax.ShapeDtypeStruct(v.shape, F32),
        compiler_params=params(20),
        cost_estimate=pl.CostEstimate(flops=3 << 29, bytes_accessed=7 << 20, transcendentals=0),
        name="first",
    )(high, low, exits, coef, v, below, above)


def gather_kernel(bv_ref, w_ref, sum_ref, low_ref, top_ref):
    levels, _, order = bv_ref.shape
    parts = order // LANES
    for m in range(levels):
        for p in range(parts):
            cols = pl.ds(p * LANES, LANES)
            s = bv_ref[m, :, cols] + 2.0 * w_ref[m * parts + p]
            sum_ref[m, :, cols] = s
            if m < 2:
                low_ref[m, :, cols] = s
            if m >= levels - 2:
                top_ref[m - levels + 2, :, cols] = s


def gather(bv, w):
    levels, rows, order = bv.shape
    edge = jax.ShapeDtypeStruct((2, rows, order), F32)
    return pl.pallas_call(
        gather_kernel,
        in_specs=[WHOLE, WHOLE],
        out_specs=[WHOLE, WHOLE, WHOLE],
        out_shape=[jax.ShapeDtypeStruct(bv.shape, F32), edge, edge],
        compiler_params=params(12),
        cost_estimate=pl.CostEstimate(flops=1 << 20, bytes_accessed=4 << 20, transcendentals=0),
        name="once",
    )(bv, w)


def twice_kernel(high_ref, low_ref, exits_ref, coef_ref, v_ref, bv_ref, s_ref, step_ref, trans_ref):
    levels, rows, order = v_ref.shape
    x = halves(s_ref[...].reshape(levels * rows, order))
    scale = coef_ref[5, 0]
    for at in range(0, order, 256):
        cols = pl.ds(at, 256)
        prod = product(x, high_ref, low_ref, cols).reshape(levels, rows, 256)

        def get(n, cols=cols):
            return s_ref[n, :, cols] if 0 <= n < levels else None

        for m in range(levels):
            here = s_ref[m, :, cols]
            change = prod[m] - here * (exits_ref[:, cols] + coef_ref[4, m])
            stepped = here + scale * (change + hops(coef_ref, m, get, levels))
            once = 0.5 * (here + bv_ref[m, :, cols])
            step_ref[m, :, cols] = stepped
            trans_ref[m, :, cols] = (v_ref[m, :, cols] + once) * 0.4 + 0.2 * stepped


def twice(high, low, exits, coef, v, bv, s):
    shape = jax.ShapeDtypeStruct(v.shape, F32)
    return pl.pallas_call(
        twice_kernel,
        in_specs=[WHOLE, WHOLE, WHOLE, SCALARS, WHOLE, WHOLE, WHOLE],
        out_specs=[WHOLE, WHOLE],
        out_shape=[shape, shape],
        compiler_params=params(24),
        cost_estimate=pl.CostEstimate(flops=3 << 29, bytes_accessed=9 << 20, transcendentals=0),
        name="twice",
    )(high, low, exits, coef, v, bv, s)


def finish_kernel(coef_ref, step_ref, trans_ref, below_ref, above_ref, w_ref, out_t_ref, out_s_ref):
    levels, _, order = step_ref.shape
    parts = order // LANES
    scale = coef_ref[5, 0]
    for m in range(levels):
        for p in range(parts):
            cols = pl.ds(p * LANES, LANES)

            def get(n, cols=cols):
                if n < 0:
                    return below_ref[n + 2, :, cols]
                return above_ref[n - levels, :, cols] if n >= levels else None

            more = w_ref[m * parts + p]
            far = hops(coef_ref, m, get, levels)
            if far is not None:
                more = more + scale * far
            out_s_ref[m, :, cols] = step_ref[m, :, cols] + more
            out_t_ref[m, :, cols] = trans_ref[m, :, cols] + 0.2 * more


def finish(coef, step, trans, below, above, w):
    shape = jax.ShapeDtypeStruct(step.shape, F32)
    return pl.pallas_call(
        finish_kernel,
        in_specs=[SCALARS, WHOLE, WHOLE, WHOLE, WHOLE, WHOLE],
        out_specs=[WHOLE, WHOLE],
        out_shape=[shape, shape],
        compiler_params=params(16),
        cost_estimate=pl.CostEstimate(flops=1 << 21, bytes_accessed=6 << 20, transcendentals=0),
        name="finish",
    )(coef, step, trans, below, above, w)


def swap(chunks):
    return lax.all_to_all(chunks, "comp", split_axis=0, concat_axis=0, tiled=True)


def neighbours(low, top):
    count = lax.axis_size("ctr")
    below = lax.ppermute(top, "ctr", [(i, i + 1) for i in range(count - 1)])
    above = lax.ppermute(low, "ctr", [(i + 1, i) for i in range(count - 1)])
    return below, above


def level_coefs(level_rate, level_code, levels):
    hop = level_code - 2 + (level_code >= 2).astype(jnp.int32)
    target = jnp.arange(level_rate.shape[0], dtype=jnp.int32) + hop
    live = (target >= 0) & (target < level_rate.shape[0])
    out_rate = jnp.where(live, level_rate, F32(0.0))
    total = level_rate.shape[0]
    rows = []
    for offset in OFFSETS:
        source = jnp.pad(jnp.where(hop == offset, level_rate, F32(0.0)), 2)
        rows.append(source[2 - offset : 2 - offset + total])
    table = jnp.stack(rows + [out_rate])
    start = lax.axis_index("ctr") * levels
    return lax.dynamic_slice_in_dim(table, start, levels, axis=1), jnp.max(out_rate)


def local(initial, rates_first, blocks_first, rates_second, blocks_second, level_rate, level_code):
    levels, rows, order = initial.shape
    count = lax.axis_size("comp")
    parts = order // LANES
    chunks = initial.reshape(levels, rows, parts, LANES).transpose(0, 2, 1, 3)
    turned_mass = swap(chunks.reshape(count, rows, LANES)).reshape(order, LANES)

    below, above = neighbours(initial[:2], initial[levels - 2 :])
    sec_high, sec_low, sec_exits = expand(rates_second, blocks_second, True)
    fst_high, fst_low, fst_exits = expand(rates_first, blocks_first, False)
    table, top_rate = level_coefs(level_rate, level_code, levels)
    uniform_rate = jnp.max(fst_exits) + jnp.max(sec_exits) + top_rate
    scale = 1.0 / uniform_rate
    coef = jnp.concatenate([table, jnp.full((1, levels), scale, F32)])
    scale = scale.reshape(1)
    exits = fst_exits.reshape(1, order)
    bv = first(fst_high, fst_low, exits, coef, initial, below, above)

    w_one = turned(sec_high, sec_low, sec_exits, scale, turned_mass)
    back_one = swap(w_one.reshape(count, rows, LANES))
    w_two = turned(sec_high, sec_low, sec_exits, scale, w_one)
    back_two = swap(w_two.reshape(count, rows, LANES))

    s, low, top = gather(bv, back_one)
    s_below, s_above = neighbours(low, top)
    step, trans = twice(fst_high, fst_low, exits, coef, initial, bv, s)
    transient, stepped = finish(coef, step, trans, s_below, s_above, back_two)
    return transient, stepped


def solution(mesh):
    placed = (P("ctr", "comp", None), P(), P(), P(), P(), P(), P())
    return jax.shard_map(
        local,
        mesh=mesh,
        in_specs=placed,
        out_specs=(P("ctr", "comp", None), P("ctr", "comp", None)),
        check_vma=False,
    )
```

```python
import functools

import jax
import jax.numpy as jnp
from jax import lax
from jax.experimental import pallas as pl
from jax.experimental.pallas import tpu as pltpu
from jax.sharding import PartitionSpec as P

F32 = jnp.float32
BF16 = jnp.bfloat16
LANES = 256
SIDE = 4
OFFSETS = (-2, -1, 1, 2)
HBM = pl.BlockSpec(memory_space=pltpu.HBM)
WHOLE = pl.BlockSpec(memory_space=pltpu.VMEM)
SCALARS = pl.BlockSpec(memory_space=pltpu.SMEM)


def params(mib):
    return pltpu.CompilerParams(vmem_limit_bytes=mib << 20)


def halves(x):
    high = x.astype(BF16)
    return high, (x - high.astype(F32)).astype(BF16)


def mm(a, b):
    return jnp.dot(a, b, preferred_element_type=F32)


def mask_rows(blocks_ref, row, tall, order):
    nblk = blocks_ref.shape[0]
    left = (row == lax.broadcasted_iota(jnp.int32, (tall, nblk), 1)).astype(BF16)
    col = lax.broadcasted_iota(jnp.int32, (nblk, order), 1) // (order // nblk)
    right = (col == lax.broadcasted_iota(jnp.int32, (nblk, order), 0)).astype(BF16)
    wide = mm(blocks_ref[...].astype(F32).astype(BF16), right).astype(BF16)
    return mm(left, wide)


def coefficients(rate_ref, code_ref, rate_row_ref, code_row_ref, start_ref, tops, coef_ref):
    total = rate_row_ref.shape[1]
    levels = coef_ref.shape[1]
    start = start_ref[0]
    code = code_row_ref[...]
    target = lax.broadcasted_iota(jnp.int32, code.shape, 1) + code - 2 + (code >= 2).astype(jnp.int32)
    live = (target >= 0) & (target < total)
    top = jnp.max(jnp.where(live, rate_row_ref[...], F32(0.0)))
    scale = 1.0 / (tops[0] + tops[1] + top)

    def hop(n):
        return code_ref[n] - 2 + jnp.where(code_ref[n] >= 2, 1, 0)

    for m in range(levels):
        here = start + m
        for k, offset in enumerate(OFFSETS):
            n = here - offset
            at = jnp.clip(n, 0, total - 1)
            good = (n >= 0) & (n < total) & (hop(at) == offset)
            coef_ref[k, m] = jnp.where(good, rate_ref[at], F32(0.0))
        to = here + hop(here)
        coef_ref[4, m] = jnp.where((to >= 0) & (to < total), rate_ref[here], F32(0.0))
        coef_ref[5, m] = scale


def prepare_kernel(
    rate_ref, code_ref, start_ref, rate_row_ref, code_row_ref, fst_ref, fst_blocks_ref, sec_ref, sec_blocks_ref,
    fst_high, fst_low, fst_exits, sec_both, sec_exits, coef_ref, tops,
):
    step = pl.program_id(0)
    tall, order = fst_ref.shape
    nblk = fst_blocks_ref.shape[0]
    width = order // nblk
    at = lax.broadcasted_iota(jnp.int32, (tall, nblk), 0)
    full = fst_ref[...] * mask_rows(fst_blocks_ref, at // width + step * (tall // width), tall, order)
    sums = jnp.sum(full, axis=1, keepdims=True)
    fst_exits[...] = jnp.broadcast_to(sums, (tall, 128)).T[:8]
    fst_high[...], fst_low[...] = halves(full)
    top_first = jnp.max(sums)

    side, along, rows, _ = sec_ref.shape
    deep = order // (side * rows)
    row = ((at // rows % side) * deep + at // (rows * side) + step * along) * rows // width
    pieces = [sec_ref[y, z] for z in range(along) for y in range(side)]
    full = jnp.concatenate(pieces, axis=0) * mask_rows(sec_blocks_ref, row, tall, order)
    sums = jnp.sum(full, axis=1, keepdims=True)
    sec_exits[:, pl.ds(pl.multiple_of(step * tall, tall), tall)] = jnp.broadcast_to(sums, (tall, 128)).T[:8]
    turn = full.T
    for z in range(deep):
        for y in range(side):
            block = turn[(y * deep + z) * rows : (y * deep + z + 1) * rows]
            to = pl.ds((z * side + y) * rows, rows)
            sec_both[0, to, :], sec_both[1, to, :] = halves(block)
    top_second = jnp.max(sums)

    @pl.when(step == 0)
    def _():
        tops[0] = top_first
        tops[1] = top_second

    @pl.when(step > 0)
    def _():
        tops[0] = jnp.maximum(tops[0], top_first)
        tops[1] = jnp.maximum(tops[1], top_second)

    @pl.when(step == pl.num_programs(0) - 1)
    def _():
        coefficients(rate_ref, code_ref, rate_row_ref, code_row_ref, start_ref, tops, coef_ref)
        sec_exits[4:8, :] = jnp.full((4, sec_exits.shape[1]), coef_ref[5, 0], F32)


def prepare(level_rate, level_code, start, rates_first, blocks_first, rates_second, blocks_second, levels, count, tall=256):
    order = rates_first.shape[0]
    total = level_rate.shape[0]
    rows = pl.BlockSpec((tall, order), lambda i: (i, 0))
    both = pl.BlockSpec((2, order, tall), lambda i: (0, 0, i))
    small = pl.BlockSpec(blocks_first.shape, lambda i: (0, 0))
    line = pl.BlockSpec((1, total), lambda i: (0, 0))
    half = jax.ShapeDtypeStruct((order, order), BF16)
    deep = count // SIDE
    along = tall // (SIDE * (order // count))
    pieces = pl.BlockSpec((SIDE, along, order // count, order), lambda i: (0, i, 0, 0))
    return pl.pallas_call(
        prepare_kernel,
        grid=(order // tall,),
        in_specs=[SCALARS, SCALARS, SCALARS, line, line, rows, small, pieces, small],
        out_specs=[
            rows, rows, pl.BlockSpec((8, tall), lambda i: (0, i)),
            both, pl.BlockSpec((8, order), lambda i: (0, 0)), SCALARS,
        ],
        out_shape=[
            half, half, jax.ShapeDtypeStruct((8, order), F32),
            jax.ShapeDtypeStruct((2, order, order), BF16),
            jax.ShapeDtypeStruct((8, order), F32), jax.ShapeDtypeStruct((6, levels), F32),
        ],
        scratch_shapes=[pltpu.SMEM((2,), F32)],
        compiler_params=params(60),
        cost_estimate=pl.CostEstimate(flops=1 << 27, bytes_accessed=16 << 20, transcendentals=0),
        name="prepare",
    )(
        level_rate, level_code, start, level_rate.reshape(1, total), level_code.reshape(1, total),
        rates_first, blocks_first, rates_second.reshape(SIDE, deep, order // count, order), blocks_second,
    )


def turned_kernel(both_ref, exits_ref, mass_ref, out_ref, up, down):
    @pl.when(pl.program_id(0) == 0)
    def _():
        up[...], down[...] = halves(mass_ref[...])

    tall = out_ref.shape[0]
    rows = pl.ds(pl.multiple_of(pl.program_id(0) * tall, tall), tall)
    left = both_ref[0]
    total = mm(left, up[...]) + mm(left, down[...]) + mm(both_ref[1], up[...])
    turn = exits_ref[...].T
    out_ref[...] = (total - mass_ref[rows, :] * turn[:, 0:1]) * turn[:, 4:5]


def turned(both, exits, mass, tall=512):
    order, width = mass.shape
    return pl.pallas_call(
        turned_kernel,
        grid=(order // tall,),
        in_specs=[
            pl.BlockSpec((2, tall, order), lambda i: (0, i, 0)),
            pl.BlockSpec((8, tall), lambda i: (0, i)),
            pl.BlockSpec((order, width), lambda i: (0, 0)),
        ],
        out_specs=pl.BlockSpec((tall, width), lambda i: (i, 0)),
        out_shape=jax.ShapeDtypeStruct(mass.shape, F32),
        scratch_shapes=[pltpu.VMEM((order, width), BF16), pltpu.VMEM((order, width), BF16)],
        compiler_params=params(60),
        cost_estimate=pl.CostEstimate(flops=3 << 29, bytes_accessed=6 << 20, transcendentals=0),
        name="second",
    )(both, exits, mass)


def product(x, high_ref, low_ref, cols):
    high, low = x
    return mm(high, high_ref[:, cols]) + mm(low, high_ref[:, cols]) + mm(high, low_ref[:, cols])


def hops(coef_ref, m, get, levels):
    total = None
    for k, offset in enumerate(OFFSETS):
        source = get(m - offset)
        if source is not None:
            part = coef_ref[k, m] * source
            total = part if total is None else total + part
    return total


def first_kernel(high_ref, low_ref, exits_ref, coef_ref, v_ref, below_ref, above_ref, out_ref):
    levels, rows, order = v_ref.shape
    x = halves(v_ref[...].reshape(levels * rows, order))
    scale = coef_ref[5, 0]
    for at in range(0, order, 256):
        cols = pl.ds(at, 256)
        prod = product(x, high_ref, low_ref, cols).reshape(levels, rows, 256)

        def get(n, cols=cols):
            if n < 0:
                return below_ref[n + 2, :, cols]
            if n >= levels:
                return above_ref[n - levels, :, cols]
            return v_ref[n, :, cols]

        for m in range(levels):
            here = v_ref[m, :, cols]
            change = prod[m] - here * (exits_ref[0:1, cols] + coef_ref[4, m])
            out_ref[m, :, cols] = here + scale * (change + hops(coef_ref, m, get, levels))


def first(high, low, exits, coef, v, below, above):
    return pl.pallas_call(
        first_kernel,
        in_specs=[WHOLE, WHOLE, WHOLE, SCALARS, WHOLE, WHOLE, WHOLE],
        out_specs=WHOLE,
        out_shape=jax.ShapeDtypeStruct(v.shape, F32),
        compiler_params=params(20),
        cost_estimate=pl.CostEstimate(flops=3 << 29, bytes_accessed=7 << 20, transcendentals=0),
        name="first",
    )(high, low, exits, coef, v, below, above)


def gather_kernel(bv_ref, w_ref, sum_ref, low_ref, top_ref):
    levels, _, order = bv_ref.shape
    parts = order // LANES
    for m in range(levels):
        for p in range(parts):
            cols = pl.ds(p * LANES, LANES)
            s = bv_ref[m, :, cols] + 2.0 * w_ref[m * parts + p]
            sum_ref[m, :, cols] = s
            if m < 2:
                low_ref[m, :, cols] = s
            if m >= levels - 2:
                top_ref[m - levels + 2, :, cols] = s


def gather(bv, w):
    levels, rows, order = bv.shape
    edge = jax.ShapeDtypeStruct((2, rows, order), F32)
    return pl.pallas_call(
        gather_kernel,
        in_specs=[WHOLE, WHOLE],
        out_specs=[WHOLE, WHOLE, WHOLE],
        out_shape=[jax.ShapeDtypeStruct(bv.shape, F32), edge, edge],
        compiler_params=params(12),
        cost_estimate=pl.CostEstimate(flops=1 << 20, bytes_accessed=4 << 20, transcendentals=0),
        name="once",
    )(bv, w)


def twice_kernel(high_ref, low_ref, exits_ref, coef_ref, v_ref, bv_ref, s_ref, below_ref, above_ref, step_ref, trans_ref):
    levels, rows, order = v_ref.shape
    x = halves(s_ref[...].reshape(levels * rows, order))
    scale = coef_ref[5, 0]
    for at in range(0, order, 256):
        cols = pl.ds(at, 256)
        prod = product(x, high_ref, low_ref, cols).reshape(levels, rows, 256)

        def get(n, cols=cols):
            if n < 0:
                return below_ref[n + 2, :, cols]
            if n >= levels:
                return above_ref[n - levels, :, cols]
            return s_ref[n, :, cols]

        for m in range(levels):
            here = s_ref[m, :, cols]
            change = prod[m] - here * (exits_ref[0:1, cols] + coef_ref[4, m])
            stepped = here + scale * (change + hops(coef_ref, m, get, levels))
            once = 0.5 * (here + bv_ref[m, :, cols])
            step_ref[m, :, cols] = stepped
            trans_ref[m, :, cols] = (v_ref[m, :, cols] + once) * 0.4 + 0.2 * stepped


def twice(high, low, exits, coef, v, bv, s, below, above):
    shape = jax.ShapeDtypeStruct(v.shape, F32)
    return pl.pallas_call(
        twice_kernel,
        in_specs=[WHOLE, WHOLE, WHOLE, SCALARS, WHOLE, WHOLE, WHOLE, WHOLE, WHOLE],
        out_specs=[WHOLE, WHOLE],
        out_shape=[shape, shape],
        compiler_params=params(24),
        cost_estimate=pl.CostEstimate(flops=3 << 29, bytes_accessed=9 << 20, transcendentals=0),
        name="twice",
    )(high, low, exits, coef, v, bv, s, below, above)


def finish_kernel(step_ref, trans_ref, w_ref, out_t_ref, out_s_ref, step, trans, sems):
    levels, _, order = step_ref.shape
    parts = order // LANES
    pairs = ((step_ref, step, out_s_ref), (trans_ref, trans, out_t_ref))
    loads = [[pltpu.make_async_copy(src.at[m], buf.at[m], sems.at[m, k]) for k, (src, buf, _) in enumerate(pairs)] for m in range(levels)]
    stores = [[pltpu.make_async_copy(buf.at[m], dst.at[m], sems.at[m, 2 + k]) for k, (_, buf, dst) in enumerate(pairs)] for m in range(levels)]
    for group in loads:
        for load in group:
            load.start()
    for m in range(levels):
        for load in loads[m]:
            load.wait()
        for p in range(parts):
            cols = pl.ds(p * LANES, LANES)
            more = w_ref[m * parts + p]
            step[m, :, cols] = step[m, :, cols] + more
            trans[m, :, cols] = trans[m, :, cols] + 0.2 * more
        for store in stores[m]:
            store.start()
    for group in stores:
        for store in group:
            store.wait()


def finish(step, trans, w):
    shape = jax.ShapeDtypeStruct(step.shape, F32)
    return pl.pallas_call(
        finish_kernel,
        in_specs=[HBM, HBM, WHOLE],
        out_specs=[HBM, HBM],
        out_shape=[shape, shape],
        scratch_shapes=[
            pltpu.VMEM(step.shape, F32),
            pltpu.VMEM(step.shape, F32),
            pltpu.SemaphoreType.DMA((step.shape[0], 4)),
        ],
        compiler_params=params(60),
        cost_estimate=pl.CostEstimate(flops=1 << 20, bytes_accessed=5 << 20, transcendentals=0),
        name="finish",
    )(step, trans, w)


def swap(chunks):
    count = lax.axis_size("comp")
    deep = count // SIDE
    order = [(p % SIDE) * deep + p // SIDE for p in range(count)]
    return lax.all_to_all(chunks, "comp", split_axis=0, concat_axis=0, axis_index_groups=[order], tiled=True)


def neighbours(low, top):
    count = lax.axis_size("ctr")
    below = lax.ppermute(top, "ctr", [(i, i + 1) for i in range(count - 1)])
    above = lax.ppermute(low, "ctr", [(i + 1, i) for i in range(count - 1)])
    return below, above


def local(initial, rates_first, blocks_first, rates_second, blocks_second, level_rate, level_code):
    levels, rows, order = initial.shape
    count = lax.axis_size("comp")
    turned_mass = swap(initial.reshape(levels, rows, order // LANES, LANES).transpose(0, 2, 1, 3).reshape(count, rows, LANES)).reshape(order, LANES)

    below, above = neighbours(initial[:2], initial[levels - 2 :])
    start = (lax.axis_index("ctr") * levels).astype(jnp.int32).reshape(1)
    fst_high, fst_low, exits, sec_both, sec_exits, coef = prepare(
        level_rate, level_code, start, rates_first, blocks_first, rates_second, blocks_second, levels, count
    )
    bv = first(fst_high, fst_low, exits, coef, initial, below, above)

    w_one = turned(sec_both, sec_exits, turned_mass)
    back_one = swap(w_one.reshape(count, rows, LANES))
    w_two = turned(sec_both, sec_exits, w_one)
    w_two, bv = lax.optimization_barrier((w_two, bv))
    back_two = swap(w_two.reshape(count, rows, LANES))

    s, low, top = gather(bv, back_one)
    s_below, s_above = neighbours(low, top)
    step, trans = twice(fst_high, fst_low, exits, coef, initial, bv, s, s_below, s_above)
    transient, stepped = finish(step, trans, back_two)
    return transient, stepped


def solution(mesh):
    placed = (P("ctr", "comp", None), P(), P(), P(), P(), P(), P())
    return jax.shard_map(
        local,
        mesh=mesh,
        in_specs=placed,
        out_specs=(P("ctr", "comp", None), P("ctr", "comp", None)),
        check_vma=False,
    )
```

```python
import functools

import jax
import jax.numpy as jnp
from jax import lax
from jax.experimental import pallas as pl
from jax.experimental.pallas import tpu as pltpu
from jax.sharding import PartitionSpec as P

F32 = jnp.float32
BF16 = jnp.bfloat16
LANES = 256
SIDE = 4
OFFSETS = (-2, -1, 1, 2)
PLANES = 17
HBM = pl.BlockSpec(memory_space=pltpu.HBM)
WHOLE = pl.BlockSpec(memory_space=pltpu.VMEM)
SCALARS = pl.BlockSpec(memory_space=pltpu.SMEM)


def params(mib):
    return pltpu.CompilerParams(vmem_limit_bytes=mib << 20)


def halves(x):
    high = x.astype(BF16)
    return high, (x - high.astype(F32)).astype(BF16)


def mm(a, b):
    return jnp.dot(a, b, preferred_element_type=F32)


def mask_rows(blocks_ref, row, tall, order):
    nblk = blocks_ref.shape[0]
    left = (row == lax.broadcasted_iota(jnp.int32, (tall, nblk), 1)).astype(BF16)
    col = lax.broadcasted_iota(jnp.int32, (nblk, order), 1) // (order // nblk)
    right = (col == lax.broadcasted_iota(jnp.int32, (nblk, order), 0)).astype(BF16)
    wide = mm(blocks_ref[...].astype(F32).astype(BF16), right).astype(BF16)
    return mm(left, wide)


def coefficients(rate_ref, code_ref, rate_row_ref, code_row_ref, start_ref, tops, coef_ref):
    total = rate_row_ref.shape[1]
    levels = coef_ref.shape[1]
    start = start_ref[0]
    code = code_row_ref[...]
    target = lax.broadcasted_iota(jnp.int32, code.shape, 1) + code - 2 + (code >= 2).astype(jnp.int32)
    live = (target >= 0) & (target < total)
    top = jnp.max(jnp.where(live, rate_row_ref[...], F32(0.0)))
    scale = 1.0 / (tops[0] + tops[1] + top)

    def hop(n):
        return code_ref[n] - 2 + jnp.where(code_ref[n] >= 2, 1, 0)

    for m in range(levels):
        here = start + m
        for k, offset in enumerate(OFFSETS):
            n = here - offset
            at = jnp.clip(n, 0, total - 1)
            good = (n >= 0) & (n < total) & (hop(at) == offset)
            coef_ref[k, m] = jnp.where(good, rate_ref[at], F32(0.0))
        to = here + hop(here)
        coef_ref[4, m] = jnp.where((to >= 0) & (to < total), rate_ref[here], F32(0.0))
        coef_ref[5, m] = scale


def prepare_kernel(
    rate_ref, code_ref, start_ref, rate_row_ref, code_row_ref, fst_ref, fst_blocks_ref, sec_ref, sec_blocks_ref,
    fst_high, fst_low, fst_exits, sec_both, sec_exits, coef_ref, tops,
):
    step = pl.program_id(0)
    tall, order = fst_ref.shape
    nblk = fst_blocks_ref.shape[0]
    width = order // nblk
    at = lax.broadcasted_iota(jnp.int32, (tall, nblk), 0)
    full = fst_ref[...] * mask_rows(fst_blocks_ref, at // width + step * (tall // width), tall, order)
    sums = jnp.sum(full, axis=1, keepdims=True)
    fst_exits[...] = jnp.broadcast_to(sums, (tall, 128)).T[:8]
    fst_high[...], fst_low[...] = halves(full)
    top_first = jnp.max(sums)

    side, along, rows, _ = sec_ref.shape
    deep = order // (side * rows)
    row = ((at // rows % side) * deep + at // (rows * side) + step * along) * rows // width
    pieces = [sec_ref[y, z] for z in range(along) for y in range(side)]
    full = jnp.concatenate(pieces, axis=0) * mask_rows(sec_blocks_ref, row, tall, order)
    sums = jnp.sum(full, axis=1, keepdims=True)
    sec_exits[:, pl.ds(pl.multiple_of(step * tall, tall), tall)] = jnp.broadcast_to(sums, (tall, 128)).T[:8]
    turn = full.T
    for z in range(deep):
        for y in range(side):
            block = turn[(y * deep + z) * rows : (y * deep + z + 1) * rows]
            to = pl.ds((z * side + y) * rows, rows)
            sec_both[0, to, :], sec_both[1, to, :] = halves(block)
    top_second = jnp.max(sums)

    @pl.when(step == 0)
    def _():
        tops[0] = top_first
        tops[1] = top_second

    @pl.when(step > 0)
    def _():
        tops[0] = jnp.maximum(tops[0], top_first)
        tops[1] = jnp.maximum(tops[1], top_second)

    @pl.when(step == pl.num_programs(0) - 1)
    def _():
        coefficients(rate_ref, code_ref, rate_row_ref, code_row_ref, start_ref, tops, coef_ref)
        sec_exits[4:8, :] = jnp.full((4, sec_exits.shape[1]), coef_ref[5, 0], F32)


def prepare(level_rate, level_code, start, rates_first, blocks_first, rates_second, blocks_second, levels, count, tall=256):
    order = rates_first.shape[0]
    total = level_rate.shape[0]
    rows = pl.BlockSpec((tall, order), lambda i: (i, 0))
    both = pl.BlockSpec((2, order, tall), lambda i: (0, 0, i))
    small = pl.BlockSpec(blocks_first.shape, lambda i: (0, 0))
    line = pl.BlockSpec((1, total), lambda i: (0, 0))
    half = jax.ShapeDtypeStruct((order, order), BF16)
    deep = count // SIDE
    along = tall // (SIDE * (order // count))
    pieces = pl.BlockSpec((SIDE, along, order // count, order), lambda i: (0, i, 0, 0))
    return pl.pallas_call(
        prepare_kernel,
        grid=(order // tall,),
        in_specs=[SCALARS, SCALARS, SCALARS, line, line, rows, small, pieces, small],
        out_specs=[
            rows, rows, pl.BlockSpec((8, tall), lambda i: (0, i)),
            both, pl.BlockSpec((8, order), lambda i: (0, 0)), SCALARS,
        ],
        out_shape=[
            half, half, jax.ShapeDtypeStruct((8, order), F32),
            jax.ShapeDtypeStruct((PLANES, order, order), BF16),
            jax.ShapeDtypeStruct((PLANES * order // 2, order), F32), jax.ShapeDtypeStruct((6, levels), F32),
        ],
        scratch_shapes=[pltpu.SMEM((2,), F32)],
        compiler_params=params(60),
        cost_estimate=pl.CostEstimate(flops=1 << 27, bytes_accessed=16 << 20, transcendentals=0),
        name="prepare",
    )(
        level_rate, level_code, start, level_rate.reshape(1, total), level_code.reshape(1, total),
        rates_first, blocks_first, rates_second.reshape(SIDE, deep, order // count, order), blocks_second,
    )


def pack_kernel(v_ref, out_ref):
    for p in range(out_ref.shape[1]):
        out_ref[:, p] = v_ref[:, :, pl.ds(p * LANES, LANES)]


def pack(v, tall=4):
    levels, rows, order = v.shape
    parts = order // LANES
    return pl.pallas_call(
        pack_kernel,
        grid=(levels // tall,),
        in_specs=[pl.BlockSpec((tall, rows, order), lambda i: (i, 0, 0))],
        out_specs=pl.BlockSpec((tall, parts, rows, LANES), lambda i: (i, 0, 0, 0)),
        out_shape=jax.ShapeDtypeStruct((levels, parts, rows, LANES), F32),
        compiler_params=params(62),
        cost_estimate=pl.CostEstimate(flops=0, bytes_accessed=2 << 20, transcendentals=0),
        name="pack",
    )(v)


def turned_kernel(both_ref, exits_ref, mass_ref, out_ref, up, down):
    @pl.when(pl.program_id(0) == 0)
    def _():
        up[...], down[...] = halves(mass_ref[...])

    tall = out_ref.shape[0]
    rows = pl.ds(pl.multiple_of(pl.program_id(0) * tall, tall), tall)
    left = both_ref[0]
    total = mm(left, up[...]) + mm(left, down[...]) + mm(both_ref[1], up[...])
    turn = exits_ref[...].T
    out_ref[...] = (total - mass_ref[rows, :] * turn[:, 0:1]) * turn[:, 4:5]


def turned(both, exits, mass, tall=512):
    order, width = mass.shape
    return pl.pallas_call(
        turned_kernel,
        grid=(order // tall,),
        in_specs=[
            pl.BlockSpec((2, tall, order), lambda i: (0, i, 0)),
            pl.BlockSpec((8, tall), lambda i: (0, i)),
            WHOLE,
        ],
        out_specs=pl.BlockSpec((tall, width), lambda i: (i, 0)),
        out_shape=jax.ShapeDtypeStruct(mass.shape, F32),
        scratch_shapes=[pltpu.VMEM((order, width), BF16), pltpu.VMEM((order, width), BF16)],
        compiler_params=params(32),
        cost_estimate=pl.CostEstimate(flops=3 << 29, bytes_accessed=6 << 20, transcendentals=0),
        name="second",
    )(both, exits, mass)


def product(x, high_ref, low_ref, cols):
    high, low = x
    return mm(high, high_ref[:, cols]) + mm(low, high_ref[:, cols]) + mm(high, low_ref[:, cols])


def hops(coef_ref, m, get, levels):
    total = None
    for k, offset in enumerate(OFFSETS):
        source = get(m - offset)
        if source is not None:
            part = coef_ref[k, m] * source
            total = part if total is None else total + part
    return total


def first_kernel(high_ref, low_ref, exits_ref, coef_ref, v_ref, below_ref, above_ref, out_ref):
    levels, rows, order = v_ref.shape
    x = halves(v_ref[...].reshape(levels * rows, order))
    scale = coef_ref[5, 0]
    for at in range(0, order, 256):
        cols = pl.ds(at, 256)
        prod = product(x, high_ref, low_ref, cols).reshape(levels, rows, 256)

        def get(n, cols=cols):
            if n < 0:
                return below_ref[n + 2, :, cols]
            if n >= levels:
                return above_ref[n - levels, :, cols]
            return v_ref[n, :, cols]

        for m in range(levels):
            here = v_ref[m, :, cols]
            change = prod[m] - here * (exits_ref[0:1, cols] + coef_ref[4, m])
            out_ref[m, :, cols] = here + scale * (change + hops(coef_ref, m, get, levels))


def first(high, low, exits, coef, v, below, above):
    return pl.pallas_call(
        first_kernel,
        in_specs=[WHOLE, WHOLE, WHOLE, SCALARS, WHOLE, WHOLE, WHOLE],
        out_specs=WHOLE,
        out_shape=jax.ShapeDtypeStruct(v.shape, F32),
        compiler_params=params(20),
        cost_estimate=pl.CostEstimate(flops=3 << 29, bytes_accessed=7 << 20, transcendentals=0),
        name="first",
    )(high, low, exits, coef, v, below, above)


def gather_kernel(bv_ref, w_ref, sum_ref, low_ref, top_ref):
    levels, _, order = bv_ref.shape
    parts = order // LANES
    for m in range(levels):
        for p in range(parts):
            cols = pl.ds(p * LANES, LANES)
            s = bv_ref[m, :, cols] + 2.0 * w_ref[m * parts + p]
            sum_ref[m, :, cols] = s
            if m < 2:
                low_ref[m, :, cols] = s
            if m >= levels - 2:
                top_ref[m - levels + 2, :, cols] = s


def gather(bv, w):
    levels, rows, order = bv.shape
    edge = jax.ShapeDtypeStruct((2, rows, order), F32)
    return pl.pallas_call(
        gather_kernel,
        in_specs=[WHOLE, WHOLE],
        out_specs=[WHOLE, WHOLE, WHOLE],
        out_shape=[jax.ShapeDtypeStruct(bv.shape, F32), edge, edge],
        compiler_params=params(62),
        cost_estimate=pl.CostEstimate(flops=1 << 20, bytes_accessed=4 << 20, transcendentals=0),
        name="once",
    )(bv, w)


def twice_kernel(high_ref, low_ref, exits_ref, coef_ref, v_ref, bv_ref, s_ref, below_ref, above_ref, both_ref):
    levels, rows, order = v_ref.shape
    x = halves(s_ref[...].reshape(levels * rows, order))
    scale = coef_ref[5, 0]
    for at in range(0, order, 256):
        cols = pl.ds(at, 256)
        prod = product(x, high_ref, low_ref, cols).reshape(levels, rows, 256)

        def get(n, cols=cols):
            if n < 0:
                return below_ref[n + 2, :, cols]
            if n >= levels:
                return above_ref[n - levels, :, cols]
            return s_ref[n, :, cols]

        for m in range(levels):
            here = s_ref[m, :, cols]
            change = prod[m] - here * (exits_ref[0:1, cols] + coef_ref[4, m])
            stepped = here + scale * (change + hops(coef_ref, m, get, levels))
            once = 0.5 * (here + bv_ref[m, :, cols])
            both_ref[0, m, :, cols] = stepped
            both_ref[1, m, :, cols] = (v_ref[m, :, cols] + once) * 0.4 + 0.2 * stepped


def twice(high, low, exits, coef, v, bv, s, below, above):
    return pl.pallas_call(
        twice_kernel,
        grid=(1,),
        in_specs=[WHOLE, WHOLE, WHOLE, SCALARS, WHOLE, WHOLE, WHOLE, WHOLE, WHOLE],
        out_specs=pl.BlockSpec((2, *v.shape), lambda i: (0, 0, 0, 0)),
        out_shape=jax.ShapeDtypeStruct((2 * PLANES, *v.shape), F32),
        compiler_params=params(32),
        cost_estimate=pl.CostEstimate(flops=3 << 29, bytes_accessed=9 << 20, transcendentals=0),
        name="twice",
    )(high, low, exits, coef, v, bv, s, below, above)


def finish_kernel(both_ref, w_ref, out_t_ref, out_s_ref):
    levels, _, order = out_s_ref.shape
    parts = order // LANES
    at = pl.program_id(0) * levels * parts
    for m in range(levels):
        for p in range(parts):
            cols = pl.ds(p * LANES, LANES)
            more = w_ref[at + m * parts + p]
            out_s_ref[m, :, cols] = both_ref[0, m, :, cols] + more
            out_t_ref[m, :, cols] = both_ref[1, m, :, cols] + 0.2 * more


def finish(both, w, tall=4):
    _, levels, rows, order = both.shape
    shape = jax.ShapeDtypeStruct((levels, rows, order), F32)
    block = pl.BlockSpec((tall, rows, order), lambda i: (i, 0, 0))
    return pl.pallas_call(
        finish_kernel,
        grid=(levels // tall,),
        in_specs=[pl.BlockSpec((2, tall, rows, order), lambda i: (0, i, 0, 0)), WHOLE],
        out_specs=[block, block],
        out_shape=[shape, shape],
        compiler_params=params(32),
        cost_estimate=pl.CostEstimate(flops=1 << 20, bytes_accessed=5 << 20, transcendentals=0),
        name="finish",
    )(both, w)


def swap(chunks):
    count = lax.axis_size("comp")
    deep = count // SIDE
    order = [(p % SIDE) * deep + p // SIDE for p in range(count)]
    return lax.all_to_all(chunks, "comp", split_axis=0, concat_axis=0, axis_index_groups=[order], tiled=True)


def neighbours(low, top):
    count = lax.axis_size("ctr")
    below = lax.ppermute(top, "ctr", [(i, i + 1) for i in range(count - 1)])
    above = lax.ppermute(low, "ctr", [(i + 1, i) for i in range(count - 1)])
    return below, above


def local(initial, rates_first, blocks_first, rates_second, blocks_second, level_rate, level_code):
    levels, rows, order = initial.shape
    count = lax.axis_size("comp")
    turned_mass = swap(pack(initial).reshape(count, rows, LANES)).reshape(order, LANES)

    below, above = neighbours(initial[:2], initial[levels - 2 :])
    start = (lax.axis_index("ctr") * levels).astype(jnp.int32).reshape(1)
    fst_high, fst_low, exits, sec_both, sec_exits, coef = prepare(
        level_rate, level_code, start, rates_first, blocks_first, rates_second, blocks_second, levels, count
    )

    turned_mass, below, above = lax.optimization_barrier((turned_mass, below, above))
    w_one = turned(sec_both, sec_exits, turned_mass)
    back_one = swap(w_one.reshape(count, rows, LANES))
    bv = first(fst_high, fst_low, exits, coef, initial, below, above)
    w_two = turned(sec_both, sec_exits, w_one)
    w_two, bv = lax.optimization_barrier((w_two, bv))
    back_two = swap(w_two.reshape(count, rows, LANES))

    s, low, top = gather(bv, back_one)
    s_below, s_above = neighbours(low, top)
    both = twice(fst_high, fst_low, exits, coef, initial, bv, s, s_below, s_above)
    transient, stepped = finish(both, back_two)
    return transient, stepped


def solution(mesh):
    placed = (P("ctr", "comp", None), P(), P(), P(), P(), P(), P())
    return jax.shard_map(
        local,
        mesh=mesh,
        in_specs=placed,
        out_specs=(P("ctr", "comp", None), P("ctr", "comp", None)),
        check_vma=False,
    )
```

```python
import functools

import jax
import jax.numpy as jnp
from jax import lax
from jax.experimental import pallas as pl
from jax.experimental.pallas import tpu as pltpu
from jax.sharding import PartitionSpec as P

F32 = jnp.float32
BF16 = jnp.bfloat16
LANES = 256
SIDE = 4
OFFSETS = (-2, -1, 1, 2)
PLANES = 17
HBM = pl.BlockSpec(memory_space=pltpu.HBM)
WHOLE = pl.BlockSpec(memory_space=pltpu.VMEM)
SCALARS = pl.BlockSpec(memory_space=pltpu.SMEM)


def params(mib):
    return pltpu.CompilerParams(vmem_limit_bytes=mib << 20)


def halves(x):
    high = x.astype(BF16)
    return high, (x - high.astype(F32)).astype(BF16)


def mm(a, b):
    return jnp.dot(a, b, preferred_element_type=F32)


def mask_rows(blocks_ref, row, tall, order):
    nblk = blocks_ref.shape[0]
    left = (row == lax.broadcasted_iota(jnp.int32, (tall, nblk), 1)).astype(BF16)
    col = lax.broadcasted_iota(jnp.int32, (nblk, order), 1) // (order // nblk)
    right = (col == lax.broadcasted_iota(jnp.int32, (nblk, order), 0)).astype(BF16)
    wide = mm(blocks_ref[...].astype(F32).astype(BF16), right).astype(BF16)
    return mm(left, wide)


def coefficients(rate_ref, code_ref, rate_row_ref, code_row_ref, start_ref, tops, coef_ref):
    total = rate_row_ref.shape[1]
    levels = coef_ref.shape[1]
    start = start_ref[0]
    code = code_row_ref[...]
    target = lax.broadcasted_iota(jnp.int32, code.shape, 1) + code - 2 + (code >= 2).astype(jnp.int32)
    live = (target >= 0) & (target < total)
    top = jnp.max(jnp.where(live, rate_row_ref[...], F32(0.0)))
    scale = 1.0 / (tops[0] + tops[1] + top)

    def hop(n):
        return code_ref[n] - 2 + jnp.where(code_ref[n] >= 2, 1, 0)

    for m in range(levels):
        here = start + m
        for k, offset in enumerate(OFFSETS):
            n = here - offset
            at = jnp.clip(n, 0, total - 1)
            good = (n >= 0) & (n < total) & (hop(at) == offset)
            coef_ref[k, m] = jnp.where(good, rate_ref[at], F32(0.0))
        to = here + hop(here)
        coef_ref[4, m] = jnp.where((to >= 0) & (to < total), rate_ref[here], F32(0.0))
        coef_ref[5, m] = scale


def prepare_kernel(
    rate_ref, code_ref, start_ref, rate_row_ref, code_row_ref, fst_ref, fst_blocks_ref, sec_ref, sec_blocks_ref,
    fst_high, fst_low, fst_exits, sec_both, sec_exits, coef_ref, tops,
):
    step = pl.program_id(0)
    tall, order = fst_ref.shape
    nblk = fst_blocks_ref.shape[0]
    width = order // nblk
    at = lax.broadcasted_iota(jnp.int32, (tall, nblk), 0)
    full = fst_ref[...] * mask_rows(fst_blocks_ref, at // width + step * (tall // width), tall, order)
    sums = jnp.sum(full, axis=1, keepdims=True)
    fst_exits[...] = jnp.broadcast_to(sums, (tall, 128)).T[:8]
    fst_high[...], fst_low[...] = halves(full)
    top_first = jnp.max(sums)

    side, along, rows, _ = sec_ref.shape
    deep = order // (side * rows)
    row = ((at // rows % side) * deep + at // (rows * side) + step * along) * rows // width
    pieces = [sec_ref[y, z] for z in range(along) for y in range(side)]
    full = jnp.concatenate(pieces, axis=0) * mask_rows(sec_blocks_ref, row, tall, order)
    sums = jnp.sum(full, axis=1, keepdims=True)
    sec_exits[:, pl.ds(pl.multiple_of(step * tall, tall), tall)] = jnp.broadcast_to(sums, (tall, 128)).T[:8]
    turn = full.T
    for z in range(deep):
        for y in range(side):
            block = turn[(y * deep + z) * rows : (y * deep + z + 1) * rows]
            to = pl.ds((z * side + y) * rows, rows)
            sec_both[0, to, :], sec_both[1, to, :] = halves(block)
    top_second = jnp.max(sums)

    @pl.when(step == 0)
    def _():
        tops[0] = top_first
        tops[1] = top_second

    @pl.when(step > 0)
    def _():
        tops[0] = jnp.maximum(tops[0], top_first)
        tops[1] = jnp.maximum(tops[1], top_second)

    @pl.when(step == pl.num_programs(0) - 1)
    def _():
        coefficients(rate_ref, code_ref, rate_row_ref, code_row_ref, start_ref, tops, coef_ref)
        sec_exits[4:8, :] = jnp.full((4, sec_exits.shape[1]), coef_ref[5, 0], F32)


def prepare(level_rate, level_code, start, rates_first, blocks_first, rates_second, blocks_second, levels, count, tall=256):
    order = rates_first.shape[0]
    total = level_rate.shape[0]
    rows = pl.BlockSpec((tall, order), lambda i: (i, 0))
    both = pl.BlockSpec((2, order, tall), lambda i: (0, 0, i))
    small = pl.BlockSpec(blocks_first.shape, lambda i: (0, 0))
    line = pl.BlockSpec((1, total), lambda i: (0, 0))
    half = jax.ShapeDtypeStruct((order, order), BF16)
    deep = count // SIDE
    along = tall // (SIDE * (order // count))
    pieces = pl.BlockSpec((SIDE, along, order // count, order), lambda i: (0, i, 0, 0))
    return pl.pallas_call(
        prepare_kernel,
        grid=(order // tall,),
        in_specs=[SCALARS, SCALARS, SCALARS, line, line, rows, small, pieces, small],
        out_specs=[
            rows, rows, pl.BlockSpec((8, tall), lambda i: (0, i)),
            both, pl.BlockSpec((8, order), lambda i: (0, 0)), SCALARS,
        ],
        out_shape=[
            half, half, jax.ShapeDtypeStruct((8, order), F32),
            jax.ShapeDtypeStruct((PLANES, order, order), BF16),
            jax.ShapeDtypeStruct((PLANES * order // 2, order), F32), jax.ShapeDtypeStruct((6, levels), F32),
        ],
        scratch_shapes=[pltpu.SMEM((2,), F32)],
        compiler_params=params(60),
        cost_estimate=pl.CostEstimate(flops=1 << 27, bytes_accessed=16 << 20, transcendentals=0),
        name="prepare",
    )(
        level_rate, level_code, start, level_rate.reshape(1, total), level_code.reshape(1, total),
        rates_first, blocks_first, rates_second.reshape(SIDE, deep, order // count, order), blocks_second,
    )


def pack_kernel(v_ref, out_ref):
    for p in range(out_ref.shape[1]):
        out_ref[:, p] = v_ref[:, :, pl.ds(p * LANES, LANES)]


def pack(v, tall=4):
    levels, rows, order = v.shape
    parts = order // LANES
    return pl.pallas_call(
        pack_kernel,
        grid=(levels // tall,),
        in_specs=[pl.BlockSpec((tall, rows, order), lambda i: (i, 0, 0))],
        out_specs=pl.BlockSpec((tall, parts, rows, LANES), lambda i: (i, 0, 0, 0)),
        out_shape=jax.ShapeDtypeStruct((levels, parts, rows, LANES), F32),
        compiler_params=params(62),
        cost_estimate=pl.CostEstimate(flops=0, bytes_accessed=2 << 20, transcendentals=0),
        name="pack",
    )(v)


def turned_kernel(both_ref, exits_ref, mass_ref, out_ref, up, down):
    @pl.when(pl.program_id(0) == 0)
    def _():
        up[...], down[...] = halves(mass_ref[...])

    tall = out_ref.shape[0]
    rows = pl.ds(pl.multiple_of(pl.program_id(0) * tall, tall), tall)
    left = both_ref[0]
    total = mm(left, up[...]) + mm(left, down[...]) + mm(both_ref[1], up[...])
    turn = exits_ref[...].T
    out_ref[...] = (total - mass_ref[rows, :] * turn[:, 0:1]) * turn[:, 4:5]


def turned(both, exits, mass, tall=512):
    order, width = mass.shape
    return pl.pallas_call(
        turned_kernel,
        grid=(order // tall,),
        in_specs=[
            pl.BlockSpec((2, tall, order), lambda i: (0, i, 0)),
            pl.BlockSpec((8, tall), lambda i: (0, i)),
            WHOLE,
        ],
        out_specs=pl.BlockSpec((tall, width), lambda i: (i, 0)),
        out_shape=jax.ShapeDtypeStruct(mass.shape, F32),
        scratch_shapes=[pltpu.VMEM((order, width), BF16), pltpu.VMEM((order, width), BF16)],
        compiler_params=params(32),
        cost_estimate=pl.CostEstimate(flops=3 << 29, bytes_accessed=6 << 20, transcendentals=0),
        name="second",
    )(both, exits, mass)


def product(x, high_ref, low_ref, cols):
    high, low = x
    return mm(high, high_ref[:, cols]) + mm(low, high_ref[:, cols]) + mm(high, low_ref[:, cols])


def hops(coef_ref, m, get, levels):
    total = None
    for k, offset in enumerate(OFFSETS):
        source = get(m - offset)
        if source is not None:
            part = coef_ref[k, m] * source
            total = part if total is None else total + part
    return total


def first_kernel(high_ref, low_ref, exits_ref, coef_ref, v_ref, below_ref, above_ref, out_ref):
    levels, rows, order = v_ref.shape
    x = halves(v_ref[...].reshape(levels * rows, order))
    scale = coef_ref[5, 0]
    for at in range(0, order, 256):
        cols = pl.ds(at, 256)
        prod = product(x, high_ref, low_ref, cols).reshape(levels, rows, 256)

        def get(n, cols=cols):
            if n < 0:
                return below_ref[n + 2, :, cols]
            if n >= levels:
                return above_ref[n - levels, :, cols]
            return v_ref[n, :, cols]

        for m in range(levels):
            here = v_ref[m, :, cols]
            change = prod[m] - here * (exits_ref[0:1, cols] + coef_ref[4, m])
            out_ref[m, :, cols] = here + scale * (change + hops(coef_ref, m, get, levels))


def first(high, low, exits, coef, v, below, above):
    return pl.pallas_call(
        first_kernel,
        grid=(1,),
        in_specs=[WHOLE, WHOLE, WHOLE, SCALARS, WHOLE, WHOLE, WHOLE],
        out_specs=pl.BlockSpec(v.shape, lambda i: (0, 0, 0)),
        out_shape=jax.ShapeDtypeStruct((2 * PLANES * v.shape[0], *v.shape[1:]), F32),
        compiler_params=params(32),
        cost_estimate=pl.CostEstimate(flops=3 << 29, bytes_accessed=7 << 20, transcendentals=0),
        name="first",
    )(high, low, exits, coef, v, below, above)


def gather_kernel(bv_ref, w_ref, sum_ref, low_ref, top_ref):
    levels, _, order = sum_ref.shape
    parts = order // LANES
    for m in range(levels):
        for p in range(parts):
            cols = pl.ds(p * LANES, LANES)
            s = bv_ref[m, :, cols] + 2.0 * w_ref[m * parts + p]
            sum_ref[m, :, cols] = s
            if m < 2:
                low_ref[m, :, cols] = s
            if m >= levels - 2:
                top_ref[m - levels + 2, :, cols] = s


def gather(bv, w, levels):
    _, rows, order = bv.shape
    whole = (levels, rows, order)
    edge = jax.ShapeDtypeStruct((2, rows, order), F32)
    return pl.pallas_call(
        gather_kernel,
        grid=(1,),
        in_specs=[pl.BlockSpec(whole, lambda i: (0, 0, 0)), WHOLE],
        out_specs=[WHOLE, WHOLE, WHOLE],
        out_shape=[jax.ShapeDtypeStruct(whole, F32), edge, edge],
        compiler_params=params(32),
        cost_estimate=pl.CostEstimate(flops=1 << 20, bytes_accessed=4 << 20, transcendentals=0),
        name="once",
    )(bv, w)


def twice_kernel(high_ref, low_ref, exits_ref, coef_ref, v_ref, bv_ref, s_ref, below_ref, above_ref, both_ref):
    levels, rows, order = v_ref.shape
    x = halves(s_ref[...].reshape(levels * rows, order))
    scale = coef_ref[5, 0]
    for at in range(0, order, 256):
        cols = pl.ds(at, 256)
        prod = product(x, high_ref, low_ref, cols).reshape(levels, rows, 256)

        def get(n, cols=cols):
            if n < 0:
                return below_ref[n + 2, :, cols]
            if n >= levels:
                return above_ref[n - levels, :, cols]
            return s_ref[n, :, cols]

        for m in range(levels):
            here = s_ref[m, :, cols]
            change = prod[m] - here * (exits_ref[0:1, cols] + coef_ref[4, m])
            stepped = here + scale * (change + hops(coef_ref, m, get, levels))
            once = 0.5 * (here + bv_ref[m, :, cols])
            both_ref[0, m, :, cols] = stepped
            both_ref[1, m, :, cols] = (v_ref[m, :, cols] + once) * 0.4 + 0.2 * stepped


def twice(high, low, exits, coef, v, bv, s, below, above):
    return pl.pallas_call(
        twice_kernel,
        grid=(1,),
        in_specs=[WHOLE, WHOLE, WHOLE, SCALARS, WHOLE, pl.BlockSpec(v.shape, lambda i: (0, 0, 0)), WHOLE, WHOLE, WHOLE],
        out_specs=pl.BlockSpec((2, *v.shape), lambda i: (0, 0, 0, 0)),
        out_shape=jax.ShapeDtypeStruct((2 * PLANES, *v.shape), F32),
        compiler_params=params(32),
        cost_estimate=pl.CostEstimate(flops=3 << 29, bytes_accessed=9 << 20, transcendentals=0),
        name="twice",
    )(high, low, exits, coef, v, bv, s, below, above)


def finish_kernel(both_ref, w_ref, out_t_ref, out_s_ref):
    levels, _, order = out_s_ref.shape
    parts = order // LANES
    for m in range(levels):
        for p in range(parts):
            cols = pl.ds(p * LANES, LANES)
            more = w_ref[m * parts + p]
            out_s_ref[m, :, cols] = both_ref[0, m, :, cols] + more
            out_t_ref[m, :, cols] = both_ref[1, m, :, cols] + 0.2 * more


def finish(both, w, tall=4):
    _, levels, rows, order = both.shape
    shape = jax.ShapeDtypeStruct((levels, rows, order), F32)
    block = pl.BlockSpec((tall, rows, order), lambda i: (i, 0, 0))
    return pl.pallas_call(
        finish_kernel,
        grid=(levels // tall,),
        in_specs=[
            pl.BlockSpec((2, tall, rows, order), lambda i: (0, i, 0, 0)),
            pl.BlockSpec((tall * (order // LANES), rows, LANES), lambda i: (i, 0, 0)),
        ],
        out_specs=[block, block],
        out_shape=[shape, shape],
        compiler_params=params(32),
        cost_estimate=pl.CostEstimate(flops=1 << 20, bytes_accessed=5 << 20, transcendentals=0),
        name="finish",
    )(both, w)


def swap(chunks):
    count = lax.axis_size("comp")
    deep = count // SIDE
    order = [(p % SIDE) * deep + p // SIDE for p in range(count)]
    return lax.all_to_all(chunks, "comp", split_axis=0, concat_axis=0, axis_index_groups=[order], tiled=True)


def neighbours(low, top):
    count = lax.axis_size("ctr")
    below = lax.ppermute(top, "ctr", [(i, i + 1) for i in range(count - 1)])
    above = lax.ppermute(low, "ctr", [(i + 1, i) for i in range(count - 1)])
    return below, above


def local(initial, rates_first, blocks_first, rates_second, blocks_second, level_rate, level_code):
    levels, rows, order = initial.shape
    count = lax.axis_size("comp")
    turned_mass = swap(pack(initial).reshape(count, rows, LANES)).reshape(order, LANES)

    below, above = neighbours(initial[:2], initial[levels - 2 :])
    start = (lax.axis_index("ctr") * levels).astype(jnp.int32).reshape(1)
    fst_high, fst_low, exits, sec_both, sec_exits, coef = prepare(
        level_rate, level_code, start, rates_first, blocks_first, rates_second, blocks_second, levels, count
    )

    turned_mass, below, above = lax.optimization_barrier((turned_mass, below, above))
    w_one = turned(sec_both, sec_exits, turned_mass)
    back_one = swap(w_one.reshape(count, rows, LANES))
    bv = first(fst_high, fst_low, exits, coef, initial, below, above)
    w_two = turned(sec_both, sec_exits, w_one)
    w_two, bv = lax.optimization_barrier((w_two, bv))
    back_two = swap(w_two.reshape(count, rows, LANES))

    s, low, top = gather(bv, back_one, levels)
    s_below, s_above = neighbours(low, top)
    both = twice(fst_high, fst_low, exits, coef, initial, bv, s, s_below, s_above)
    transient, stepped = finish(both, back_two)
    return transient, stepped


def solution(mesh):
    placed = (P("ctr", "comp", None), P(), P(), P(), P(), P(), P())
    return jax.shard_map(
        local,
        mesh=mesh,
        in_specs=placed,
        out_specs=(P("ctr", "comp", None), P("ctr", "comp", None)),
        check_vma=False,
    )
```

```python
import functools

import jax
import jax.numpy as jnp
from jax import lax
from jax.experimental import pallas as pl
from jax.experimental.pallas import tpu as pltpu
from jax.sharding import PartitionSpec as P

F32 = jnp.float32
BF16 = jnp.bfloat16
LANES = 256
SIDE = 4
OFFSETS = (-2, -1, 1, 2)
PLANES = 17
HBM = pl.BlockSpec(memory_space=pltpu.HBM)
WHOLE = pl.BlockSpec(memory_space=pltpu.VMEM)
SCALARS = pl.BlockSpec(memory_space=pltpu.SMEM)


def params(mib):
    return pltpu.CompilerParams(vmem_limit_bytes=mib << 20)


def halves(x):
    high = x.astype(BF16)
    return high, (x - high.astype(F32)).astype(BF16)


def mm(a, b):
    return jnp.dot(a, b, preferred_element_type=F32)


def mask_rows(blocks_ref, row, tall, order):
    nblk = blocks_ref.shape[0]
    left = (row == lax.broadcasted_iota(jnp.int32, (tall, nblk), 1)).astype(BF16)
    col = lax.broadcasted_iota(jnp.int32, (nblk, order), 1) // (order // nblk)
    right = (col == lax.broadcasted_iota(jnp.int32, (nblk, order), 0)).astype(BF16)
    wide = mm(blocks_ref[...].astype(F32).astype(BF16), right).astype(BF16)
    return mm(left, wide)


def coefficients(rate_ref, code_ref, rate_row_ref, code_row_ref, start_ref, tops, coef_ref):
    total = rate_row_ref.shape[1]
    levels = coef_ref.shape[1]
    start = start_ref[0]
    code = code_row_ref[...]
    target = lax.broadcasted_iota(jnp.int32, code.shape, 1) + code - 2 + (code >= 2).astype(jnp.int32)
    live = (target >= 0) & (target < total)
    top = jnp.max(jnp.where(live, rate_row_ref[...], F32(0.0)))
    scale = 1.0 / (tops[0] + tops[1] + top)

    def hop(n):
        return code_ref[n] - 2 + jnp.where(code_ref[n] >= 2, 1, 0)

    for m in range(levels):
        here = start + m
        for k, offset in enumerate(OFFSETS):
            n = here - offset
            at = jnp.clip(n, 0, total - 1)
            good = (n >= 0) & (n < total) & (hop(at) == offset)
            coef_ref[k, m] = jnp.where(good, rate_ref[at], F32(0.0))
        to = here + hop(here)
        coef_ref[4, m] = jnp.where((to >= 0) & (to < total), rate_ref[here], F32(0.0))
        coef_ref[5, m] = scale


def prepare_kernel(
    rate_ref, code_ref, start_ref, rate_row_ref, code_row_ref, fst_ref, fst_blocks_ref, sec_ref, sec_blocks_ref,
    fst_high, fst_low, fst_exits, sec_both, sec_exits, coef_ref, tops,
):
    step = pl.program_id(0)
    tall, order = fst_ref.shape
    nblk = fst_blocks_ref.shape[0]
    width = order // nblk
    at = lax.broadcasted_iota(jnp.int32, (tall, nblk), 0)
    full = fst_ref[...] * mask_rows(fst_blocks_ref, at // width + step * (tall // width), tall, order)
    sums = jnp.sum(full, axis=1, keepdims=True)
    fst_exits[...] = jnp.broadcast_to(sums, (tall, 128)).T[:8]
    fst_high[...], fst_low[...] = halves(full)
    top_first = jnp.max(sums)

    side, along, rows, _ = sec_ref.shape
    deep = order // (side * rows)
    row = ((at // rows % side) * deep + at // (rows * side) + step * along) * rows // width
    pieces = [sec_ref[y, z] for z in range(along) for y in range(side)]
    full = jnp.concatenate(pieces, axis=0) * mask_rows(sec_blocks_ref, row, tall, order)
    sums = jnp.sum(full, axis=1, keepdims=True)
    sec_exits[:, pl.ds(pl.multiple_of(step * tall, tall), tall)] = jnp.broadcast_to(sums, (tall, 128)).T[:8]
    turn = full.T
    for z in range(deep):
        for y in range(side):
            block = turn[(y * deep + z) * rows : (y * deep + z + 1) * rows]
            to = pl.ds((z * side + y) * rows, rows)
            sec_both[0, to, :], sec_both[1, to, :] = halves(block)
    top_second = jnp.max(sums)

    @pl.when(step == 0)
    def _():
        tops[0] = top_first
        tops[1] = top_second

    @pl.when(step > 0)
    def _():
        tops[0] = jnp.maximum(tops[0], top_first)
        tops[1] = jnp.maximum(tops[1], top_second)

    @pl.when(step == pl.num_programs(0) - 1)
    def _():
        coefficients(rate_ref, code_ref, rate_row_ref, code_row_ref, start_ref, tops, coef_ref)
        sec_exits[4:8, :] = jnp.full((4, sec_exits.shape[1]), coef_ref[5, 0], F32)


def prepare(level_rate, level_code, start, rates_first, blocks_first, rates_second, blocks_second, levels, count, tall=256):
    order = rates_first.shape[0]
    total = level_rate.shape[0]
    rows = pl.BlockSpec((tall, order), lambda i: (i, 0))
    both = pl.BlockSpec((2, order, tall), lambda i: (0, 0, i))
    small = pl.BlockSpec(blocks_first.shape, lambda i: (0, 0))
    line = pl.BlockSpec((1, total), lambda i: (0, 0))
    half = jax.ShapeDtypeStruct((order, order), BF16)
    deep = count // SIDE
    along = tall // (SIDE * (order // count))
    pieces = pl.BlockSpec((SIDE, along, order // count, order), lambda i: (0, i, 0, 0))
    return pl.pallas_call(
        prepare_kernel,
        grid=(order // tall,),
        in_specs=[SCALARS, SCALARS, SCALARS, line, line, rows, small, pieces, small],
        out_specs=[
            rows, rows, pl.BlockSpec((8, tall), lambda i: (0, i)),
            both, pl.BlockSpec((8, order), lambda i: (0, 0)), SCALARS,
        ],
        out_shape=[
            half, half, jax.ShapeDtypeStruct((8, order), F32),
            jax.ShapeDtypeStruct((PLANES, order, order), BF16),
            jax.ShapeDtypeStruct((PLANES * order // 2, order), F32), jax.ShapeDtypeStruct((6, levels), F32),
        ],
        scratch_shapes=[pltpu.SMEM((2,), F32)],
        compiler_params=params(60),
        cost_estimate=pl.CostEstimate(flops=1 << 27, bytes_accessed=16 << 20, transcendentals=0),
        name="prepare",
    )(
        level_rate, level_code, start, level_rate.reshape(1, total), level_code.reshape(1, total),
        rates_first, blocks_first, rates_second.reshape(SIDE, deep, order // count, order), blocks_second,
    )


def pack_kernel(v_ref, out_ref):
    for p in range(out_ref.shape[1]):
        out_ref[:, p] = v_ref[:, :, pl.ds(p * LANES, LANES)]


def pack(v, tall=4):
    levels, rows, order = v.shape
    parts = order // LANES
    return pl.pallas_call(
        pack_kernel,
        grid=(levels // tall,),
        in_specs=[pl.BlockSpec((tall, rows, order), lambda i: (i, 0, 0))],
        out_specs=pl.BlockSpec((tall, parts, rows, LANES), lambda i: (i, 0, 0, 0)),
        out_shape=jax.ShapeDtypeStruct((levels, parts, rows, LANES), F32),
        compiler_params=params(62),
        cost_estimate=pl.CostEstimate(flops=0, bytes_accessed=2 << 20, transcendentals=0),
        name="pack",
    )(v)


def turned_kernel(high_ref, low_ref, exits_ref, mass_ref, out_ref, up, down):
    @pl.when(pl.program_id(0) == 0)
    def _():
        up[...], down[...] = halves(mass_ref[...])

    tall = out_ref.shape[0]
    rows = pl.ds(pl.multiple_of(pl.program_id(0) * tall, tall), tall)
    left = high_ref[0]
    total = mm(left, up[...]) + mm(left, down[...]) + mm(low_ref[0], up[...])
    turn = exits_ref[...].T
    out_ref[...] = (total - mass_ref[rows, :] * turn[:, 0:1]) * turn[:, 4:5]


def turned(both, exits, mass, tall=512):
    order, width = mass.shape
    return pl.pallas_call(
        turned_kernel,
        grid=(order // tall,),
        in_specs=[
            pl.BlockSpec((1, tall, order), lambda i: (0, i, 0)),
            pl.BlockSpec((1, tall, order), lambda i: (1, i, 0)),
            pl.BlockSpec((8, tall), lambda i: (0, i)),
            WHOLE,
        ],
        out_specs=pl.BlockSpec((tall, width), lambda i: (i, 0)),
        out_shape=jax.ShapeDtypeStruct(mass.shape, F32),
        scratch_shapes=[pltpu.VMEM((order, width), BF16), pltpu.VMEM((order, width), BF16)],
        compiler_params=params(32),
        cost_estimate=pl.CostEstimate(flops=3 << 29, bytes_accessed=6 << 20, transcendentals=0),
        name="second",
    )(both, both, exits, mass)


def product(x, high_ref, low_ref, cols):
    high, low = x
    return mm(high, high_ref[:, cols]) + mm(low, high_ref[:, cols]) + mm(high, low_ref[:, cols])


def hops(coef_ref, m, get, levels):
    total = None
    for k, offset in enumerate(OFFSETS):
        source = get(m - offset)
        if source is not None:
            part = coef_ref[k, m] * source
            total = part if total is None else total + part
    return total


def first_kernel(high_ref, low_ref, exits_ref, coef_ref, v_ref, below_ref, above_ref, out_ref):
    levels, rows, order = v_ref.shape
    x = halves(v_ref[...].reshape(levels * rows, order))
    scale = coef_ref[5, 0]
    for at in range(0, order, 256):
        cols = pl.ds(at, 256)
        prod = product(x, high_ref, low_ref, cols).reshape(levels, rows, 256)

        def get(n, cols=cols):
            if n < 0:
                return below_ref[n + 2, :, cols]
            if n >= levels:
                return above_ref[n - levels, :, cols]
            return v_ref[n, :, cols]

        for m in range(levels):
            here = v_ref[m, :, cols]
            change = prod[m] - here * (exits_ref[0:1, cols] + coef_ref[4, m])
            out_ref[m, :, cols] = here + scale * (change + hops(coef_ref, m, get, levels))


def first(high, low, exits, coef, v, below, above):
    return pl.pallas_call(
        first_kernel,
        grid=(1,),
        in_specs=[WHOLE, WHOLE, WHOLE, SCALARS, WHOLE, WHOLE, WHOLE],
        out_specs=pl.BlockSpec(v.shape, lambda i: (0, 0, 0)),
        out_shape=jax.ShapeDtypeStruct((2 * PLANES * v.shape[0], *v.shape[1:]), F32),
        compiler_params=params(32),
        cost_estimate=pl.CostEstimate(flops=3 << 29, bytes_accessed=7 << 20, transcendentals=0),
        name="first",
    )(high, low, exits, coef, v, below, above)


def gather_kernel(bv_ref, w_ref, sum_ref, low_ref, top_ref):
    levels, _, order = sum_ref.shape
    parts = order // LANES
    for m in range(levels):
        for p in range(parts):
            cols = pl.ds(p * LANES, LANES)
            s = bv_ref[m, :, cols] + 2.0 * w_ref[m * parts + p]
            sum_ref[m, :, cols] = s
            if m < 2:
                low_ref[m, :, cols] = s
            if m >= levels - 2:
                top_ref[m - levels + 2, :, cols] = s


def gather(bv, w, levels):
    _, rows, order = bv.shape
    whole = (levels, rows, order)
    edge = jax.ShapeDtypeStruct((2, rows, order), F32)
    return pl.pallas_call(
        gather_kernel,
        grid=(1,),
        in_specs=[pl.BlockSpec(whole, lambda i: (0, 0, 0)), WHOLE],
        out_specs=[WHOLE, WHOLE, WHOLE],
        out_shape=[jax.ShapeDtypeStruct(whole, F32), edge, edge],
        compiler_params=params(32),
        cost_estimate=pl.CostEstimate(flops=1 << 20, bytes_accessed=4 << 20, transcendentals=0),
        name="once",
    )(bv, w)


def twice_kernel(high_ref, low_ref, exits_ref, coef_ref, v_ref, bv_ref, s_ref, below_ref, above_ref, both_ref):
    levels, rows, order = v_ref.shape
    x = halves(s_ref[...].reshape(levels * rows, order))
    scale = coef_ref[5, 0]
    for at in range(0, order, 256):
        cols = pl.ds(at, 256)
        prod = product(x, high_ref, low_ref, cols).reshape(levels, rows, 256)

        def get(n, cols=cols):
            if n < 0:
                return below_ref[n + 2, :, cols]
            if n >= levels:
                return above_ref[n - levels, :, cols]
            return s_ref[n, :, cols]

        for m in range(levels):
            here = s_ref[m, :, cols]
            change = prod[m] - here * (exits_ref[0:1, cols] + coef_ref[4, m])
            stepped = here + scale * (change + hops(coef_ref, m, get, levels))
            once = 0.5 * (here + bv_ref[m, :, cols])
            both_ref[0, m, :, cols] = stepped
            both_ref[1, m, :, cols] = (v_ref[m, :, cols] + once) * 0.4 + 0.2 * stepped


def twice(high, low, exits, coef, v, bv, s, below, above):
    return pl.pallas_call(
        twice_kernel,
        grid=(1,),
        in_specs=[WHOLE, WHOLE, WHOLE, SCALARS, WHOLE, pl.BlockSpec(v.shape, lambda i: (0, 0, 0)), WHOLE, WHOLE, WHOLE],
        out_specs=pl.BlockSpec((2, *v.shape), lambda i: (0, 0, 0, 0)),
        out_shape=jax.ShapeDtypeStruct((2 * PLANES, *v.shape), F32),
        compiler_params=params(32),
        cost_estimate=pl.CostEstimate(flops=3 << 29, bytes_accessed=9 << 20, transcendentals=0),
        name="twice",
    )(high, low, exits, coef, v, bv, s, below, above)


def finish_kernel(step_ref, trans_ref, w_ref, out_t_ref, out_s_ref):
    levels, _, order = out_s_ref.shape
    parts = order // LANES
    for m in range(levels):
        for p in range(parts):
            cols = pl.ds(p * LANES, LANES)
            more = w_ref[m * parts + p]
            out_s_ref[m, :, cols] = step_ref[0, m, :, cols] + more
            out_t_ref[m, :, cols] = trans_ref[0, m, :, cols] + 0.2 * more


def finish(both, w, tall=4):
    _, levels, rows, order = both.shape
    shape = jax.ShapeDtypeStruct((levels, rows, order), F32)
    block = pl.BlockSpec((tall, rows, order), lambda i: (i, 0, 0))
    return pl.pallas_call(
        finish_kernel,
        grid=(levels // tall,),
        in_specs=[
            pl.BlockSpec((1, tall, rows, order), lambda i: (0, i, 0, 0)),
            pl.BlockSpec((1, tall, rows, order), lambda i: (1, i, 0, 0)),
            pl.BlockSpec((tall * (order // LANES), rows, LANES), lambda i: (i, 0, 0)),
        ],
        out_specs=[block, block],
        out_shape=[shape, shape],
        compiler_params=params(32),
        cost_estimate=pl.CostEstimate(flops=1 << 20, bytes_accessed=5 << 20, transcendentals=0),
        name="finish",
    )(both, both, w)


def swap(chunks):
    count = lax.axis_size("comp")
    deep = count // SIDE
    order = [(p % SIDE) * deep + p // SIDE for p in range(count)]
    return lax.all_to_all(chunks, "comp", split_axis=0, concat_axis=0, axis_index_groups=[order], tiled=True)


def neighbours(low, top):
    count = lax.axis_size("ctr")
    below = lax.ppermute(top, "ctr", [(i, i + 1) for i in range(count - 1)])
    above = lax.ppermute(low, "ctr", [(i + 1, i) for i in range(count - 1)])
    return below, above


def local(initial, rates_first, blocks_first, rates_second, blocks_second, level_rate, level_code):
    levels, rows, order = initial.shape
    count = lax.axis_size("comp")
    turned_mass = swap(pack(initial).reshape(count, rows, LANES)).reshape(order, LANES)

    below, above = neighbours(initial[:2], initial[levels - 2 :])
    start = (lax.axis_index("ctr") * levels).astype(jnp.int32).reshape(1)
    fst_high, fst_low, exits, sec_both, sec_exits, coef = prepare(
        level_rate, level_code, start, rates_first, blocks_first, rates_second, blocks_second, levels, count
    )

    turned_mass, below, above = lax.optimization_barrier((turned_mass, below, above))
    w_one = turned(sec_both, sec_exits, turned_mass)
    back_one = swap(w_one.reshape(count, rows, LANES))
    bv = first(fst_high, fst_low, exits, coef, initial, below, above)
    w_two = turned(sec_both, sec_exits, w_one)
    w_two, bv = lax.optimization_barrier((w_two, bv))
    back_two = swap(w_two.reshape(count, rows, LANES))

    s, low, top = gather(bv, back_one, levels)
    s_below, s_above = neighbours(low, top)
    both = twice(fst_high, fst_low, exits, coef, initial, bv, s, s_below, s_above)
    transient, stepped = finish(both, back_two)
    return transient, stepped


def solution(mesh):
    placed = (P("ctr", "comp", None), P(), P(), P(), P(), P(), P())
    return jax.shard_map(
        local,
        mesh=mesh,
        in_specs=placed,
        out_specs=(P("ctr", "comp", None), P("ctr", "comp", None)),
        check_vma=False,
    )
```

```python
import functools

import jax
import jax.numpy as jnp
from jax import lax
from jax.experimental import pallas as pl
from jax.experimental.pallas import tpu as pltpu
from jax.sharding import PartitionSpec as P

F32 = jnp.float32
BF16 = jnp.bfloat16
LANES = 256
SIDE = 4
OFFSETS = (-2, -1, 1, 2)
PLANES = 17
HBM = pl.BlockSpec(memory_space=pltpu.HBM)
WHOLE = pl.BlockSpec(memory_space=pltpu.VMEM)
SCALARS = pl.BlockSpec(memory_space=pltpu.SMEM)


def params(mib):
    return pltpu.CompilerParams(vmem_limit_bytes=mib << 20)


def halves(x):
    high = x.astype(BF16)
    return high, (x - high.astype(F32)).astype(BF16)


def mm(a, b):
    return jnp.dot(a, b, preferred_element_type=F32)


def mask_rows(blocks_ref, row, tall, order):
    nblk = blocks_ref.shape[0]
    left = (row == lax.broadcasted_iota(jnp.int32, (tall, nblk), 1)).astype(BF16)
    col = lax.broadcasted_iota(jnp.int32, (nblk, order), 1) // (order // nblk)
    right = (col == lax.broadcasted_iota(jnp.int32, (nblk, order), 0)).astype(BF16)
    wide = mm(blocks_ref[...].astype(F32).astype(BF16), right).astype(BF16)
    return mm(left, wide)


def coefficients(rate_ref, code_ref, rate_row_ref, code_row_ref, start_ref, tops, coef_ref):
    total = rate_row_ref.shape[1]
    levels = coef_ref.shape[1]
    start = start_ref[0]
    code = code_row_ref[...]
    target = lax.broadcasted_iota(jnp.int32, code.shape, 1) + code - 2 + (code >= 2).astype(jnp.int32)
    live = (target >= 0) & (target < total)
    top = jnp.max(jnp.where(live, rate_row_ref[...], F32(0.0)))
    scale = 1.0 / (tops[0] + tops[1] + top)

    def hop(n):
        return code_ref[n] - 2 + jnp.where(code_ref[n] >= 2, 1, 0)

    for m in range(levels):
        here = start + m
        for k, offset in enumerate(OFFSETS):
            n = here - offset
            at = jnp.clip(n, 0, total - 1)
            good = (n >= 0) & (n < total) & (hop(at) == offset)
            coef_ref[k, m] = jnp.where(good, rate_ref[at], F32(0.0))
        to = here + hop(here)
        coef_ref[4, m] = jnp.where((to >= 0) & (to < total), rate_ref[here], F32(0.0))
        coef_ref[5, m] = scale


def prepare_kernel(
    rate_ref, code_ref, start_ref, rate_row_ref, code_row_ref, fst_ref, fst_blocks_ref, sec_ref, sec_blocks_ref,
    fst_high, fst_low, fst_exits, sec_both, sec_exits, coef_ref, tops,
):
    step = pl.program_id(0)
    tall, order = fst_ref.shape
    nblk = fst_blocks_ref.shape[0]
    width = order // nblk
    at = lax.broadcasted_iota(jnp.int32, (tall, nblk), 0)
    full = fst_ref[...] * mask_rows(fst_blocks_ref, at // width + step * (tall // width), tall, order)
    sums = jnp.sum(full, axis=1, keepdims=True)
    fst_exits[...] = jnp.broadcast_to(sums, (tall, 128)).T[:8]
    fst_high[...], fst_low[...] = halves(full)
    top_first = jnp.max(sums)

    side, along, rows, _ = sec_ref.shape
    deep = order // (side * rows)
    row = ((at // rows % side) * deep + at // (rows * side) + step * along) * rows // width
    pieces = [sec_ref[y, z] for z in range(along) for y in range(side)]
    full = jnp.concatenate(pieces, axis=0) * mask_rows(sec_blocks_ref, row, tall, order)
    sums = jnp.sum(full, axis=1, keepdims=True)
    sec_exits[:, pl.ds(pl.multiple_of(step * tall, tall), tall)] = jnp.broadcast_to(sums, (tall, 128)).T[:8]
    turn = full.T
    for z in range(deep):
        for y in range(side):
            block = turn[(y * deep + z) * rows : (y * deep + z + 1) * rows]
            to = pl.ds((z * side + y) * rows, rows)
            sec_both[0, to, :], sec_both[1, to, :] = halves(block)
    top_second = jnp.max(sums)

    @pl.when(step == 0)
    def _():
        tops[0] = top_first
        tops[1] = top_second

    @pl.when(step > 0)
    def _():
        tops[0] = jnp.maximum(tops[0], top_first)
        tops[1] = jnp.maximum(tops[1], top_second)

    @pl.when(step == pl.num_programs(0) - 1)
    def _():
        coefficients(rate_ref, code_ref, rate_row_ref, code_row_ref, start_ref, tops, coef_ref)
        sec_exits[4:8, :] = jnp.full((4, sec_exits.shape[1]), coef_ref[5, 0], F32)


def prepare(level_rate, level_code, start, rates_first, blocks_first, rates_second, blocks_second, levels, count, tall=256):
    order = rates_first.shape[0]
    total = level_rate.shape[0]
    rows = pl.BlockSpec((tall, order), lambda i: (i, 0))
    both = pl.BlockSpec((2, order, tall), lambda i: (0, 0, i))
    small = pl.BlockSpec(blocks_first.shape, lambda i: (0, 0))
    line = pl.BlockSpec((1, total), lambda i: (0, 0))
    half = jax.ShapeDtypeStruct((order, order), BF16)
    deep = count // SIDE
    along = tall // (SIDE * (order // count))
    pieces = pl.BlockSpec((SIDE, along, order // count, order), lambda i: (0, i, 0, 0))
    return pl.pallas_call(
        prepare_kernel,
        grid=(order // tall,),
        in_specs=[SCALARS, SCALARS, SCALARS, line, line, rows, small, pieces, small],
        out_specs=[
            rows, rows, pl.BlockSpec((8, tall), lambda i: (0, i)),
            both, pl.BlockSpec((8, order), lambda i: (0, 0)), SCALARS,
        ],
        out_shape=[
            half, half, jax.ShapeDtypeStruct((8, order), F32),
            jax.ShapeDtypeStruct((PLANES, order, order), BF16),
            jax.ShapeDtypeStruct((PLANES * order // 2, order), F32), jax.ShapeDtypeStruct((6, levels), F32),
        ],
        scratch_shapes=[pltpu.SMEM((2,), F32)],
        compiler_params=params(60),
        cost_estimate=pl.CostEstimate(flops=1 << 27, bytes_accessed=16 << 20, transcendentals=0),
        name="prepare",
    )(
        level_rate, level_code, start, level_rate.reshape(1, total), level_code.reshape(1, total),
        rates_first, blocks_first, rates_second.reshape(SIDE, deep, order // count, order), blocks_second,
    )


def pack_kernel(v_ref, out_ref):
    for p in range(out_ref.shape[1]):
        out_ref[:, p] = v_ref[:, :, pl.ds(p * LANES, LANES)]


def pack(v, tall=4):
    levels, rows, order = v.shape
    parts = order // LANES
    return pl.pallas_call(
        pack_kernel,
        grid=(levels // tall,),
        in_specs=[pl.BlockSpec((tall, rows, order), lambda i: (i, 0, 0))],
        out_specs=pl.BlockSpec((tall, parts, rows, LANES), lambda i: (i, 0, 0, 0)),
        out_shape=jax.ShapeDtypeStruct((levels, parts, rows, LANES), F32),
        compiler_params=params(62),
        cost_estimate=pl.CostEstimate(flops=0, bytes_accessed=2 << 20, transcendentals=0),
        name="pack",
    )(v)


def turned_kernel(both_ref, exits_ref, mass_ref, out_ref, up, down):
    @pl.when(pl.program_id(0) == 0)
    def _():
        up[...], down[...] = halves(mass_ref[...])

    tall = out_ref.shape[0]
    rows = pl.ds(pl.multiple_of(pl.program_id(0) * tall, tall), tall)
    left = both_ref[0]
    total = mm(left, up[...]) + mm(left, down[...]) + mm(both_ref[1], up[...])
    turn = exits_ref[...].T
    out_ref[...] = (total - mass_ref[rows, :] * turn[:, 0:1]) * turn[:, 4:5]


def turned(both, exits, mass, tall=512):
    order, width = mass.shape
    return pl.pallas_call(
        turned_kernel,
        grid=(order // tall,),
        in_specs=[
            pl.BlockSpec((2, tall, order), lambda i: (0, i, 0)),
            pl.BlockSpec((8, tall), lambda i: (0, i)),
            WHOLE,
        ],
        out_specs=pl.BlockSpec((tall, width), lambda i: (i, 0)),
        out_shape=jax.ShapeDtypeStruct(mass.shape, F32),
        scratch_shapes=[pltpu.VMEM((order, width), BF16), pltpu.VMEM((order, width), BF16)],
        compiler_params=params(32),
        cost_estimate=pl.CostEstimate(flops=3 << 29, bytes_accessed=6 << 20, transcendentals=0),
        name="second",
    )(both, exits, mass)


def product(x, high_ref, low_ref, cols):
    high, low = x
    return mm(high, high_ref[:, cols]) + mm(low, high_ref[:, cols]) + mm(high, low_ref[:, cols])


def hops(coef_ref, m, get, levels):
    total = None
    for k, offset in enumerate(OFFSETS):
        source = get(m - offset)
        if source is not None:
            part = coef_ref[k, m] * source
            total = part if total is None else total + part
    return total


def first_kernel(high_ref, low_ref, exits_ref, coef_ref, v_ref, below_ref, above_ref, out_ref):
    levels, rows, order = v_ref.shape
    x = halves(v_ref[...].reshape(levels * rows, order))
    scale = coef_ref[5, 0]
    for at in range(0, order, 256):
        cols = pl.ds(at, 256)
        prod = product(x, high_ref, low_ref, cols).reshape(levels, rows, 256)

        def get(n, cols=cols):
            if n < 0:
                return below_ref[n + 2, :, cols]
            if n >= levels:
                return above_ref[n - levels, :, cols]
            return v_ref[n, :, cols]

        for m in range(levels):
            here = v_ref[m, :, cols]
            change = prod[m] - here * (exits_ref[0:1, cols] + coef_ref[4, m])
            out_ref[m, :, cols] = here + scale * (change + hops(coef_ref, m, get, levels))


def first(high, low, exits, coef, v, below, above):
    return pl.pallas_call(
        first_kernel,
        grid=(1,),
        in_specs=[WHOLE, WHOLE, WHOLE, SCALARS, WHOLE, WHOLE, WHOLE],
        out_specs=pl.BlockSpec(v.shape, lambda i: (0, 0, 0)),
        out_shape=jax.ShapeDtypeStruct((2 * PLANES * v.shape[0], *v.shape[1:]), F32),
        compiler_params=params(32),
        cost_estimate=pl.CostEstimate(flops=3 << 29, bytes_accessed=7 << 20, transcendentals=0),
        name="first",
    )(high, low, exits, coef, v, below, above)


def gather_kernel(bv_ref, w_ref, sum_ref, low_ref, top_ref):
    levels, _, order = sum_ref.shape
    parts = order // LANES
    for m in range(levels):
        for p in range(parts):
            cols = pl.ds(p * LANES, LANES)
            s = bv_ref[m, :, cols] + 2.0 * w_ref[m * parts + p]
            sum_ref[m, :, cols] = s
            if m < 2:
                low_ref[m, :, cols] = s
            if m >= levels - 2:
                top_ref[m - levels + 2, :, cols] = s


def gather(bv, w, levels):
    _, rows, order = bv.shape
    whole = (levels, rows, order)
    edge = jax.ShapeDtypeStruct((2, rows, order), F32)
    return pl.pallas_call(
        gather_kernel,
        grid=(1,),
        in_specs=[pl.BlockSpec(whole, lambda i: (0, 0, 0)), WHOLE],
        out_specs=[WHOLE, WHOLE, WHOLE],
        out_shape=[jax.ShapeDtypeStruct(whole, F32), edge, edge],
        compiler_params=params(32),
        cost_estimate=pl.CostEstimate(flops=1 << 20, bytes_accessed=4 << 20, transcendentals=0),
        name="once",
    )(bv, w)


def twice_kernel(high_ref, low_ref, exits_ref, coef_ref, v_ref, bv_ref, s_ref, below_ref, above_ref, both_ref):
    levels, rows, order = v_ref.shape
    x = halves(s_ref[...].reshape(levels * rows, order))
    scale = coef_ref[5, 0]
    for at in range(0, order, 256):
        cols = pl.ds(at, 256)
        prod = product(x, high_ref, low_ref, cols).reshape(levels, rows, 256)

        def get(n, cols=cols):
            if n < 0:
                return below_ref[n + 2, :, cols]
            if n >= levels:
                return above_ref[n - levels, :, cols]
            return s_ref[n, :, cols]

        for m in range(levels):
            here = s_ref[m, :, cols]
            change = prod[m] - here * (exits_ref[0:1, cols] + coef_ref[4, m])
            stepped = here + scale * (change + hops(coef_ref, m, get, levels))
            once = 0.5 * (here + bv_ref[m, :, cols])
            both_ref[0, m, :, cols] = stepped
            both_ref[1, m, :, cols] = (v_ref[m, :, cols] + once) * 0.4 + 0.2 * stepped


def twice(high, low, exits, coef, v, bv, s, below, above):
    return pl.pallas_call(
        twice_kernel,
        grid=(1,),
        in_specs=[WHOLE, WHOLE, WHOLE, SCALARS, WHOLE, pl.BlockSpec(v.shape, lambda i: (0, 0, 0)), WHOLE, WHOLE, WHOLE],
        out_specs=pl.BlockSpec((2, *v.shape), lambda i: (0, 0, 0, 0)),
        out_shape=jax.ShapeDtypeStruct((2 * PLANES, *v.shape), F32),
        compiler_params=params(32),
        cost_estimate=pl.CostEstimate(flops=3 << 29, bytes_accessed=9 << 20, transcendentals=0),
        name="twice",
    )(high, low, exits, coef, v, bv, s, below, above)


def finish_kernel(both_ref, w_ref, out_t_ref, out_s_ref):
    levels, _, order = out_s_ref.shape
    parts = order // LANES
    for m in range(levels):
        for p in range(parts):
            cols = pl.ds(p * LANES, LANES)
            more = w_ref[m * parts + p]
            out_s_ref[m, :, cols] = both_ref[0, m, :, cols] + more
            out_t_ref[m, :, cols] = both_ref[1, m, :, cols] + 0.2 * more


def finish(both, w, tall=4):
    _, levels, rows, order = both.shape
    shape = jax.ShapeDtypeStruct((levels, rows, order), F32)
    block = pl.BlockSpec((tall, rows, order), lambda i: (i, 0, 0))
    return pl.pallas_call(
        finish_kernel,
        grid=(levels // tall,),
        in_specs=[
            pl.BlockSpec((2, tall, rows, order), lambda i: (0, i, 0, 0)),
            pl.BlockSpec((tall * (order // LANES), rows, LANES), lambda i: (i, 0, 0)),
        ],
        out_specs=[block, block],
        out_shape=[shape, shape],
        compiler_params=params(32),
        cost_estimate=pl.CostEstimate(flops=1 << 20, bytes_accessed=5 << 20, transcendentals=0),
        name="finish",
    )(both, w)


def swap(chunks):
    count = lax.axis_size("comp")
    deep = count // SIDE
    order = [(p % SIDE) * deep + p // SIDE for p in range(count)]
    return lax.all_to_all(chunks, "comp", split_axis=0, concat_axis=0, axis_index_groups=[order], tiled=True)


def neighbours(low, top):
    count = lax.axis_size("ctr")
    below = lax.ppermute(top, "ctr", [(i, i + 1) for i in range(count - 1)])
    above = lax.ppermute(low, "ctr", [(i + 1, i) for i in range(count - 1)])
    return below, above


def local(initial, rates_first, blocks_first, rates_second, blocks_second, level_rate, level_code):
    levels, rows, order = initial.shape
    count = lax.axis_size("comp")
    turned_mass = swap(pack(initial).reshape(count, rows, LANES)).reshape(order, LANES)

    below, above = neighbours(initial[:2], initial[levels - 2 :])
    start = (lax.axis_index("ctr") * levels).astype(jnp.int32).reshape(1)
    fst_high, fst_low, exits, sec_both, sec_exits, coef = prepare(
        level_rate, level_code, start, rates_first, blocks_first, rates_second, blocks_second, levels, count
    )

    w_one = turned(sec_both, sec_exits, turned_mass)
    back_one = swap(w_one.reshape(count, rows, LANES))
    bv = first(fst_high, fst_low, exits, coef, initial, below, above)
    w_two = turned(sec_both, sec_exits, w_one)
    w_two, bv = lax.optimization_barrier((w_two, bv))
    back_two = swap(w_two.reshape(count, rows, LANES))

    s, low, top = gather(bv, back_one, levels)
    s_below, s_above = neighbours(low, top)
    both = twice(fst_high, fst_low, exits, coef, initial, bv, s, s_below, s_above)
    transient, stepped = finish(both, back_two)
    return transient, stepped


def solution(mesh):
    placed = (P("ctr", "comp", None), P(), P(), P(), P(), P(), P())
    return jax.shard_map(
        local,
        mesh=mesh,
        in_specs=placed,
        out_specs=(P("ctr", "comp", None), P("ctr", "comp", None)),
        check_vma=False,
    )
```

```python
import functools

import jax
import jax.numpy as jnp
from jax import lax
from jax.experimental import pallas as pl
from jax.experimental.pallas import tpu as pltpu
from jax.sharding import PartitionSpec as P

F32 = jnp.float32
BF16 = jnp.bfloat16
LANES = 256
SIDE = 4
OFFSETS = (-2, -1, 1, 2)
PLANES = 17
HBM = pl.BlockSpec(memory_space=pltpu.HBM)
WHOLE = pl.BlockSpec(memory_space=pltpu.VMEM)
SCALARS = pl.BlockSpec(memory_space=pltpu.SMEM)


def params(mib):
    return pltpu.CompilerParams(vmem_limit_bytes=mib << 20)


def halves(x):
    high = x.astype(BF16)
    return high, (x - high.astype(F32)).astype(BF16)


def mm(a, b):
    return jnp.dot(a, b, preferred_element_type=F32)


def mask_rows(blocks_ref, row, tall, order):
    nblk = blocks_ref.shape[0]
    left = (row == lax.broadcasted_iota(jnp.int32, (tall, nblk), 1)).astype(BF16)
    col = lax.broadcasted_iota(jnp.int32, (nblk, order), 1) // (order // nblk)
    right = (col == lax.broadcasted_iota(jnp.int32, (nblk, order), 0)).astype(BF16)
    wide = mm(blocks_ref[...].astype(F32).astype(BF16), right).astype(BF16)
    return mm(left, wide)


def coefficients(rate_ref, code_ref, rate_row_ref, code_row_ref, start_ref, tops, coef_ref):
    total = rate_row_ref.shape[1]
    levels = coef_ref.shape[1]
    start = start_ref[0]
    code = code_row_ref[...]
    target = lax.broadcasted_iota(jnp.int32, code.shape, 1) + code - 2 + (code >= 2).astype(jnp.int32)
    live = (target >= 0) & (target < total)
    top = jnp.max(jnp.where(live, rate_row_ref[...], F32(0.0)))
    scale = 1.0 / (tops[0] + tops[1] + top)

    def hop(n):
        return code_ref[n] - 2 + jnp.where(code_ref[n] >= 2, 1, 0)

    for m in range(levels):
        here = start + m
        for k, offset in enumerate(OFFSETS):
            n = here - offset
            at = jnp.clip(n, 0, total - 1)
            good = (n >= 0) & (n < total) & (hop(at) == offset)
            coef_ref[k, m] = jnp.where(good, rate_ref[at], F32(0.0))
        to = here + hop(here)
        coef_ref[4, m] = jnp.where((to >= 0) & (to < total), rate_ref[here], F32(0.0))
        coef_ref[5, m] = scale


def prepare_kernel(
    rate_ref, code_ref, start_ref, rate_row_ref, code_row_ref, fst_ref, fst_blocks_ref, sec_ref, sec_blocks_ref,
    fst_high, fst_low, fst_exits, sec_both, sec_exits, coef_ref, tops,
):
    step = pl.program_id(0)
    tall, order = fst_ref.shape
    nblk = fst_blocks_ref.shape[0]
    width = order // nblk
    at = lax.broadcasted_iota(jnp.int32, (tall, nblk), 0)
    full = fst_ref[...] * mask_rows(fst_blocks_ref, at // width + step * (tall // width), tall, order)
    sums = jnp.sum(full, axis=1, keepdims=True)
    fst_exits[...] = jnp.broadcast_to(sums, (tall, 128)).T[:8]
    fst_high[...], fst_low[...] = halves(full)
    top_first = jnp.max(sums)

    side, along, rows, _ = sec_ref.shape
    deep = order // (side * rows)
    row = ((at // rows % side) * deep + at // (rows * side) + step * along) * rows // width
    pieces = [sec_ref[y, z] for z in range(along) for y in range(side)]
    full = jnp.concatenate(pieces, axis=0) * mask_rows(sec_blocks_ref, row, tall, order)
    sums = jnp.sum(full, axis=1, keepdims=True)
    sec_exits[:, pl.ds(pl.multiple_of(step * tall, tall), tall)] = jnp.broadcast_to(sums, (tall, 128)).T[:8]
    turn = full.T
    for z in range(deep):
        for y in range(side):
            block = turn[(y * deep + z) * rows : (y * deep + z + 1) * rows]
            to = pl.ds((z * side + y) * rows, rows)
            sec_both[0, to, :], sec_both[1, to, :] = halves(block)
    top_second = jnp.max(sums)

    @pl.when(step == 0)
    def _():
        tops[0] = top_first
        tops[1] = top_second

    @pl.when(step > 0)
    def _():
        tops[0] = jnp.maximum(tops[0], top_first)
        tops[1] = jnp.maximum(tops[1], top_second)

    @pl.when(step == pl.num_programs(0) - 1)
    def _():
        coefficients(rate_ref, code_ref, rate_row_ref, code_row_ref, start_ref, tops, coef_ref)
        sec_exits[4:8, :] = jnp.full((4, sec_exits.shape[1]), coef_ref[5, 0], F32)


def prepare(level_rate, level_code, start, rates_first, blocks_first, rates_second, blocks_second, levels, count, tall=256):
    order = rates_first.shape[0]
    total = level_rate.shape[0]
    rows = pl.BlockSpec((tall, order), lambda i: (i, 0))
    both = pl.BlockSpec((2, order, tall), lambda i: (0, 0, i))
    small = pl.BlockSpec(blocks_first.shape, lambda i: (0, 0))
    line = pl.BlockSpec((1, total), lambda i: (0, 0))
    half = jax.ShapeDtypeStruct((order, order), BF16)
    deep = count // SIDE
    along = tall // (SIDE * (order // count))
    pieces = pl.BlockSpec((SIDE, along, order // count, order), lambda i: (0, i, 0, 0))
    return pl.pallas_call(
        prepare_kernel,
        grid=(order // tall,),
        in_specs=[SCALARS, SCALARS, SCALARS, line, line, rows, small, pieces, small],
        out_specs=[
            rows, rows, pl.BlockSpec((8, tall), lambda i: (0, i)),
            both, pl.BlockSpec((8, order), lambda i: (0, 0)), SCALARS,
        ],
        out_shape=[
            half, half, jax.ShapeDtypeStruct((8, order), F32),
            jax.ShapeDtypeStruct((PLANES, order, order), BF16),
            jax.ShapeDtypeStruct((PLANES * order // 2, order), F32), jax.ShapeDtypeStruct((6, levels), F32),
        ],
        scratch_shapes=[pltpu.SMEM((2,), F32)],
        compiler_params=params(60),
        cost_estimate=pl.CostEstimate(flops=1 << 27, bytes_accessed=16 << 20, transcendentals=0),
        name="prepare",
    )(
        level_rate, level_code, start, level_rate.reshape(1, total), level_code.reshape(1, total),
        rates_first, blocks_first, rates_second.reshape(SIDE, deep, order // count, order), blocks_second,
    )


def pack_kernel(v_ref, out_ref):
    for p in range(out_ref.shape[1]):
        out_ref[:, p] = v_ref[:, :, pl.ds(p * LANES, LANES)]


def pack(v, tall=4):
    levels, rows, order = v.shape
    parts = order // LANES
    return pl.pallas_call(
        pack_kernel,
        grid=(levels // tall,),
        in_specs=[pl.BlockSpec((tall, rows, order), lambda i: (i, 0, 0))],
        out_specs=pl.BlockSpec((tall, parts, rows, LANES), lambda i: (i, 0, 0, 0)),
        out_shape=jax.ShapeDtypeStruct((levels, parts, rows, LANES), F32),
        compiler_params=params(62),
        cost_estimate=pl.CostEstimate(flops=0, bytes_accessed=2 << 20, transcendentals=0),
        name="pack",
    )(v)


def turned_kernel(high_ref, low_ref, exits_ref, mass_ref, out_ref, up, down):
    @pl.when(pl.program_id(0) == 0)
    def _():
        up[...], down[...] = halves(mass_ref[...])

    tall = out_ref.shape[0]
    rows = pl.ds(pl.multiple_of(pl.program_id(0) * tall, tall), tall)
    left = high_ref[0]
    total = mm(left, up[...]) + mm(left, down[...]) + mm(low_ref[0], up[...])
    turn = exits_ref[...].T
    out_ref[...] = (total - mass_ref[rows, :] * turn[:, 0:1]) * turn[:, 4:5]


def turned(both, exits, mass, tall=512):
    order, width = mass.shape
    return pl.pallas_call(
        turned_kernel,
        grid=(order // tall,),
        in_specs=[
            pl.BlockSpec((1, tall, order), lambda i: (0, i, 0)),
            pl.BlockSpec((1, tall, order), lambda i: (1, i, 0)),
            pl.BlockSpec((8, tall), lambda i: (0, i)),
            WHOLE,
        ],
        out_specs=pl.BlockSpec((tall, width), lambda i: (i, 0)),
        out_shape=jax.ShapeDtypeStruct(mass.shape, F32),
        scratch_shapes=[pltpu.VMEM((order, width), BF16), pltpu.VMEM((order, width), BF16)],
        compiler_params=params(32),
        cost_estimate=pl.CostEstimate(flops=3 << 29, bytes_accessed=6 << 20, transcendentals=0),
        name="second",
    )(both, both, exits, mass)


def product(x, high_ref, low_ref, cols):
    high, low = x
    return mm(high, high_ref[:, cols]) + mm(low, high_ref[:, cols]) + mm(high, low_ref[:, cols])


def hops(coef_ref, m, get, levels):
    total = None
    for k, offset in enumerate(OFFSETS):
        source = get(m - offset)
        if source is not None:
            part = coef_ref[k, m] * source
            total = part if total is None else total + part
    return total


def first_kernel(high_ref, low_ref, exits_ref, coef_ref, v_ref, below_ref, above_ref, out_ref):
    levels, rows, order = v_ref.shape
    x = halves(v_ref[...].reshape(levels * rows, order))
    scale = coef_ref[5, 0]
    for at in range(0, order, 256):
        cols = pl.ds(at, 256)
        prod = product(x, high_ref, low_ref, cols).reshape(levels, rows, 256)

        def get(n, cols=cols):
            if n < 0:
                return below_ref[n + 2, :, cols]
            if n >= levels:
                return above_ref[n - levels, :, cols]
            return v_ref[n, :, cols]

        for m in range(levels):
            here = v_ref[m, :, cols]
            change = prod[m] - here * (exits_ref[0:1, cols] + coef_ref[4, m])
            out_ref[m, :, cols] = here + scale * (change + hops(coef_ref, m, get, levels))


def first(high, low, exits, coef, v, below, above):
    return pl.pallas_call(
        first_kernel,
        grid=(1,),
        in_specs=[WHOLE, WHOLE, WHOLE, SCALARS, WHOLE, WHOLE, WHOLE],
        out_specs=pl.BlockSpec(v.shape, lambda i: (0, 0, 0)),
        out_shape=jax.ShapeDtypeStruct((2 * PLANES * v.shape[0], *v.shape[1:]), F32),
        compiler_params=params(32),
        cost_estimate=pl.CostEstimate(flops=3 << 29, bytes_accessed=7 << 20, transcendentals=0),
        name="first",
    )(high, low, exits, coef, v, below, above)


def gather_kernel(bv_ref, w_ref, sum_ref, low_ref, top_ref):
    levels, _, order = sum_ref.shape
    parts = order // LANES
    for m in range(levels):
        for p in range(parts):
            cols = pl.ds(p * LANES, LANES)
            s = bv_ref[m, :, cols] + 2.0 * w_ref[m * parts + p]
            sum_ref[m, :, cols] = s
            if m < 2:
                low_ref[m, :, cols] = s
            if m >= levels - 2:
                top_ref[m - levels + 2, :, cols] = s


def gather(bv, w, levels):
    _, rows, order = bv.shape
    whole = (levels, rows, order)
    edge = jax.ShapeDtypeStruct((2, rows, order), F32)
    return pl.pallas_call(
        gather_kernel,
        grid=(1,),
        in_specs=[pl.BlockSpec(whole, lambda i: (0, 0, 0)), WHOLE],
        out_specs=[WHOLE, WHOLE, WHOLE],
        out_shape=[jax.ShapeDtypeStruct(whole, F32), edge, edge],
        compiler_params=params(32),
        cost_estimate=pl.CostEstimate(flops=1 << 20, bytes_accessed=4 << 20, transcendentals=0),
        name="once",
    )(bv, w)


def twice_kernel(high_ref, low_ref, exits_ref, coef_ref, v_ref, bv_ref, s_ref, below_ref, above_ref, both_ref):
    levels, rows, order = v_ref.shape
    x = halves(s_ref[...].reshape(levels * rows, order))
    scale = coef_ref[5, 0]
    for at in range(0, order, 256):
        cols = pl.ds(at, 256)
        prod = product(x, high_ref, low_ref, cols).reshape(levels, rows, 256)

        def get(n, cols=cols):
            if n < 0:
                return below_ref[n + 2, :, cols]
            if n >= levels:
                return above_ref[n - levels, :, cols]
            return s_ref[n, :, cols]

        for m in range(levels):
            here = s_ref[m, :, cols]
            change = prod[m] - here * (exits_ref[0:1, cols] + coef_ref[4, m])
            stepped = here + scale * (change + hops(coef_ref, m, get, levels))
            once = 0.5 * (here + bv_ref[m, :, cols])
            both_ref[0, m, :, cols] = stepped
            both_ref[1, m, :, cols] = (v_ref[m, :, cols] + once) * 0.4 + 0.2 * stepped


def twice(high, low, exits, coef, v, bv, s, below, above):
    return pl.pallas_call(
        twice_kernel,
        grid=(1,),
        in_specs=[WHOLE, WHOLE, WHOLE, SCALARS, WHOLE, pl.BlockSpec(v.shape, lambda i: (0, 0, 0)), WHOLE, WHOLE, WHOLE],
        out_specs=pl.BlockSpec((2, *v.shape), lambda i: (0, 0, 0, 0)),
        out_shape=jax.ShapeDtypeStruct((2 * PLANES, *v.shape), F32),
        compiler_params=params(32),
        cost_estimate=pl.CostEstimate(flops=3 << 29, bytes_accessed=9 << 20, transcendentals=0),
        name="twice",
    )(high, low, exits, coef, v, bv, s, below, above)


def finish_kernel(step_ref, trans_ref, w_ref, out_t_ref, out_s_ref):
    levels, _, order = out_s_ref.shape
    parts = order // LANES
    at = pl.program_id(0) * levels * parts
    for m in range(levels):
        for p in range(parts):
            cols = pl.ds(p * LANES, LANES)
            more = w_ref[at + m * parts + p]
            out_s_ref[m, :, cols] = step_ref[0, m, :, cols] + more
            out_t_ref[m, :, cols] = trans_ref[0, m, :, cols] + 0.2 * more


def finish(both, w, tall=4):
    _, levels, rows, order = both.shape
    shape = jax.ShapeDtypeStruct((levels, rows, order), F32)
    block = pl.BlockSpec((tall, rows, order), lambda i: (i, 0, 0))
    return pl.pallas_call(
        finish_kernel,
        grid=(levels // tall,),
        in_specs=[
            pl.BlockSpec((1, tall, rows, order), lambda i: (0, i, 0, 0)),
            pl.BlockSpec((1, tall, rows, order), lambda i: (1, i, 0, 0)),
            WHOLE,
        ],
        out_specs=[block, block],
        out_shape=[shape, shape],
        compiler_params=params(32),
        cost_estimate=pl.CostEstimate(flops=1 << 20, bytes_accessed=5 << 20, transcendentals=0),
        name="finish",
    )(both, both, w)


def swap(chunks):
    count = lax.axis_size("comp")
    deep = count // SIDE
    order = [(p % SIDE) * deep + p // SIDE for p in range(count)]
    return lax.all_to_all(chunks, "comp", split_axis=0, concat_axis=0, axis_index_groups=[order], tiled=True)


def neighbours(low, top):
    count = lax.axis_size("ctr")
    below = lax.ppermute(top, "ctr", [(i, i + 1) for i in range(count - 1)])
    above = lax.ppermute(low, "ctr", [(i + 1, i) for i in range(count - 1)])
    return below, above


def local(initial, rates_first, blocks_first, rates_second, blocks_second, level_rate, level_code):
    levels, rows, order = initial.shape
    count = lax.axis_size("comp")
    turned_mass = swap(pack(initial).reshape(count, rows, LANES)).reshape(order, LANES)

    below, above = neighbours(initial[:2], initial[levels - 2 :])
    start = (lax.axis_index("ctr") * levels).astype(jnp.int32).reshape(1)
    fst_high, fst_low, exits, sec_both, sec_exits, coef = prepare(
        level_rate, level_code, start, rates_first, blocks_first, rates_second, blocks_second, levels, count
    )

    turned_mass, below, above = lax.optimization_barrier((turned_mass, below, above))
    w_one = turned(sec_both, sec_exits, turned_mass)
    back_one = swap(w_one.reshape(count, rows, LANES))
    bv = first(fst_high, fst_low, exits, coef, initial, below, above)
    w_two = turned(sec_both, sec_exits, w_one)
    w_two, bv = lax.optimization_barrier((w_two, bv))
    back_two = swap(w_two.reshape(count, rows, LANES))

    s, low, top = gather(bv, back_one, levels)
    s_below, s_above = neighbours(low, top)
    both = twice(fst_high, fst_low, exits, coef, initial, bv, s, s_below, s_above)
    transient, stepped = finish(both, back_two)
    return transient, stepped


def solution(mesh):
    placed = (P("ctr", "comp", None), P(), P(), P(), P(), P(), P())
    return jax.shard_map(
        local,
        mesh=mesh,
        in_specs=placed,
        out_specs=(P("ctr", "comp", None), P("ctr", "comp", None)),
        check_vma=False,
    )
```
